128 devices in a mesh: grp: 4 (over y_lo, core), slab: 32 (over z, x, y_hi).
Axes of the slice: x: 4, y: 4 (y_hi: 2, y_lo: 2; y = y_hi * 2 + y_lo), z: 4, core: 2. Of those that a mesh axis runs over, the one named last changes fastest.
Arguments:
- velocity: float32 [3, 128, 144, 512], P(None, 'slab', None, 'grp'), may hold values from -6 to 6
- w_in: bfloat16 [27, 16, 3], replicated, may hold values from -0.625 to 0.625
- w_mid_a: bfloat16 [27, 16, 16], replicated, may hold values from -0.3125 to 0.3125
- w_mid_b: bfloat16 [27, 16, 16], replicated, may hold values from -0.3125 to 0.3125
- w_out: bfloat16 [27, 6, 16], replicated, may hold values from -0.3125 to 0.3125
Outputs:
- velocity_next: float32 [3, 128, 144, 512], P(None, 'slab', None, 'grp')
- stress: bfloat16 [6, 64, 72, 256], P(None, 'slab', 'grp')
- grad_in: float32 [27, 16, 3], replicated
- grad_mid_a: float32 [27, 16, 16], replicated
- grad_mid_b: float32 [27, 16, 16], replicated
- grad_out: float32 [27, 6, 16], replicated
The draws below stay inside these ranges and needn't reach their ends.
All inputs are finite; a program needn't handle non-finite values.
Results may differ from the reference program's by a relative error of at most 0.0071.
Values may be sent and summed in bfloat16 or wider, within the bound.
A program may use at most 448 MiB of HBM per device.

```python
import jax
import jax.numpy as jnp
from jax import lax

C = 16
NY = 144
NX = 128
NZ = 512


def shard_levels(stream_key, extent, shards, least, largest):
    def one(axis_at, shards_of):
        heights = jax.random.uniform(jax.random.fold_in(jax.random.fold_in(stream_key, 6), axis_at), (shards_of,), jnp.float32, least / len(shards), largest / len(shards))
        return jnp.repeat(jnp.exp(heights), extent[axis_at] // shards_of).reshape((-1,) + (1,) * (len(extent) - axis_at - 1))

    level = one(*shards[0])
    for cut in shards[1:]:
        level = level * one(*cut)
    return level


def gaussian(rng, shape, scale, reach, cuts=(), kind=jnp.bfloat16):
    loudness = shard_levels(rng, shape, cuts, -0.22, 0.18) if cuts else 1.0
    array = jax.random.normal(rng, shape, jnp.float32) * scale * loudness
    return jnp.minimum(jnp.maximum(array, -reach), reach).astype(kind)


def setup_inputs(seed: int = 0) -> dict:
    keys = jax.random.split(jax.random.key(seed), 6)
    velocity = gaussian(keys[0], (3, NX, NY, NZ), 1.0, 6.0, ((1, 32), (3, 4)), jnp.float32)
    w_in = gaussian(keys[1], (27, C, 3), (27 * 3) ** -0.5, 0.625)
    w_mid_a = gaussian(keys[2], (27, C, C), (27 * C) ** -0.5, 0.3125)
    w_mid_b = gaussian(keys[3], (27, C, C), (27 * C) ** -0.5, 0.3125)
    w_out = gaussian(keys[4], (27, 6, C), (27 * C) ** -0.5, 0.3125)
    return dict(velocity=velocity, w_in=w_in, w_mid_a=w_mid_a, w_mid_b=w_mid_b, w_out=w_out)


step_size = 0.1
viscosity = 0.5
closure_weight = 4.0
pair_table = ((0, 3, 4), (3, 1, 5), (4, 5, 2))
stress_pairs = ((0, 0), (1, 1), (2, 2), (0, 1), (0, 2), (1, 2))

def gradient_along(padded, along):
    length = padded.shape[along] - 4

    def window_at(offset):
        return lax.slice_in_dim(padded, offset, offset + length, axis=along)
    return (window_at(0) - 8.0 * window_at(1) + 8.0 * window_at(3) - window_at(4)) / 12.0

def laplace_along(padded, along):
    length = padded.shape[along] - 4

    def window_at(offset):
        return lax.slice_in_dim(padded, offset, offset + length, axis=along)
    return (-window_at(0) + 16.0 * window_at(1) - 30.0 * window_at(2) + 16.0 * window_at(3) - window_at(4)) / 12.0

def wall_ghosts(interior):
    return jnp.pad(interior, ((0, 0), (0, 0), (2, 2), (0, 0)))

def stress_force(extended):
    inner_x = extended[:, :, :, 2:-2]
    inner_z = extended[:, 2:-2]
    walled = wall_ghosts(extended[:, 2:-2, :, 2:-2])
    components = []
    for along_x, along_y, along_z in pair_table:
        summed = gradient_along(inner_x[along_x:along_x + 1], 1)
        summed = summed + gradient_along(walled[along_y:along_y + 1], 2)
        summed = summed + gradient_along(inner_z[along_z:along_z + 1], 3)
        components.append(-closure_weight * summed)
    return jnp.concatenate(components, axis=0)

def tendency(extended, forcing):
    inner_x = extended[:, :, :, 2:-2]
    inner_z = extended[:, 2:-2]
    interior = extended[:, 2:-2, :, 2:-2]
    walled = wall_ghosts(interior)
    advect = interior[0:1] * gradient_along(inner_x, 1)
    advect = advect + interior[1:2] * gradient_along(walled, 2)
    advect = advect + interior[2:3] * gradient_along(inner_z, 3)
    diffuse = laplace_along(inner_x, 1) + laplace_along(walled, 2) + laplace_along(inner_z, 3)
    return -advect + viscosity * diffuse + forcing

def block_mean(field):
    comps, cells_x, cells_y, cells_z = field.shape
    return field.reshape(comps, cells_x // 2, 2, cells_y // 2, 2, cells_z // 2, 2).mean(axis=(2, 4, 6))

def filter_fields(velocity):
    block_means = block_mean(velocity)
    products = jnp.stack([velocity[left_comp] * velocity[right_comp] for left_comp, right_comp in stress_pairs])
    resolved = jnp.stack([block_means[left_comp] * block_means[right_comp] for left_comp, right_comp in stress_pairs])
    return jnp.concatenate([block_means, block_mean(products) - resolved], axis=0).astype(jnp.bfloat16)

def prolong(coarse):
    return jnp.repeat(jnp.repeat(jnp.repeat(coarse, 2, axis=1), 2, axis=2), 2, axis=3)

def convolve(activation, weight):
    out_ch, in_ch = (weight.shape[1], weight.shape[2])
    padded = jnp.pad(activation, ((0, 0), (1, 1), (0, 0), (1, 1)), mode='wrap')
    padded = jnp.pad(padded, ((0, 0), (0, 0), (1, 1), (0, 0)))
    kernel = weight.reshape(3, 3, 3, out_ch, in_ch).transpose(3, 4, 0, 1, 2)
    return lax.conv_general_dilated(padded[None], kernel, (1, 1, 1), 'VALID', precision=lax.Precision.HIGHEST)[0]

def periodic_rim(field, width):
    return jnp.pad(field, ((0, 0), (width, width), (0, 0), (width, width)), mode='wrap')

def reference(velocity, w_in, w_mid_a, w_mid_b, w_out):
    coarse = filter_fields(velocity).astype(jnp.float32)
    weights = [weight.astype(jnp.float32) for weight in (w_in, w_mid_a, w_mid_b, w_out)]
    activation = coarse[:3]
    inputs = []
    response = activation
    for layer_index in range(4):
        inputs.append(activation)
        response = convolve(activation, weights[layer_index])
        if layer_index < 3:
            activation = lax.optimization_barrier(jnp.tanh(response).astype(jnp.bfloat16)).astype(jnp.float32)
    predicted = response
    stress = predicted.astype(jnp.bfloat16)
    length = 6 * predicted.shape[1] * predicted.shape[2] * predicted.shape[3]
    cotangent = (2.0 / length * (predicted - coarse[3:])).astype(jnp.bfloat16)
    cotangent = lax.optimization_barrier(cotangent).astype(jnp.float32)
    gradients = [None, None, None, None]
    for layer_index in (3, 2, 1, 0):
        unused_out, pullback = jax.vjp(convolve, inputs[layer_index], weights[layer_index])
        spread, gradients[layer_index] = pullback(cotangent)
        if layer_index > 0:
            below_act = inputs[layer_index]
            cotangent = (spread * (1.0 - below_act * below_act)).astype(jnp.bfloat16)
            cotangent = lax.optimization_barrier(cotangent).astype(jnp.float32)
    extended_tau = prolong(periodic_rim(stress.astype(jnp.float32), 1))
    forcing = stress_force(extended_tau)
    first_section = velocity + step_size * tendency(periodic_rim(velocity, 2), forcing)
    second = tendency(periodic_rim(first_section, 2), forcing)
    velocity_next = 0.5 * (velocity + first_section + step_size * second)
    return (velocity_next, stress, gradients[0], gradients[1], gradients[2], gradients[3])
```

```python
import jax
import jax.numpy as jnp
import numpy as np
from jax import lax
from jax.experimental import pallas as pl
from jax.experimental.pallas import tpu as pltpu
from jax.sharding import PartitionSpec as P

MESH = pl.DeviceIdType.MESH
F32 = jnp.float32
BF = jnp.bfloat16
GRP, SLAB = 4, 32
RY = 80
NB = 10
ROWS = NB * RY
OWN = 8 * RY
pair_table = ((0, 3, 4), (3, 1, 5), (4, 5, 2))
stress_pairs = ((0, 0), (1, 1), (2, 2), (0, 1), (0, 2), (1, 2))
SIZE = 6 * 64 * 72 * 256


def tables():
    fsel = np.zeros((256, 128), np.float32)
    for z in range(64):
        fsel[2 * z, z] = 1
        fsel[128 + 2 * z, 64 + z] = 1
    fedge = np.zeros((2, 384, 128), np.float32)
    fexp = np.zeros((256, NB * 128), np.float32)
    for f in range(3):
        for zi in range(8):
            fedge[0, f * 128 + 2 * (56 + zi), 64 + f * 8 + zi] = 1
            fedge[1, f * 128 + 2 * zi, 88 + f * 8 + zi] = 1
            fexp[192 + f * 8 + zi, zi * 16 + f] = 1
            fexp[216 + f * 8 + zi, 9 * 128 + zi * 16 + f] = 1
            for zb in range(8):
                fexp[f * 64 + zb * 8 + zi, (zb + 1) * 128 + zi * 16 + f] = 1
    texp = np.zeros((768, 1024), np.float32)
    comp = np.zeros((1024, 384), np.float32)
    cedge = np.zeros((2, 128, 128), np.float32)
    cexp = np.zeros((512, NB * 128), np.float32)
    for c in range(6):
        for zi in range(8):
            cedge[0, zi * 16 + c, c * 8 + zi] = 1
            cedge[1, zi * 16 + c, 48 + c * 8 + zi] = 1
            cexp[384 + c * 8 + zi, zi * 16 + c] = 1
            cexp[432 + c * 8 + zi, 9 * 128 + zi * 16 + c] = 1
            for zb in range(8):
                z = zb * 8 + zi
                texp[c * 128 + 2 * z, zb * 128 + zi * 16 + c] = 1
                comp[zb * 128 + zi * 16 + c, c * 64 + z] = 1
                cexp[c * 64 + z, (zb + 1) * 128 + zi * 16 + c] = 1
    vz = np.zeros((2, 1536, 128), np.float32)
    vze = np.zeros((128, 1536), np.float32)
    for p in range(12):
        for k in range(4):
            vz[0, p * 128 + 124 + k, p * 4 + k] = 1
            vz[1, p * 128 + k, 64 + p * 4 + k] = 1
            vze[p * 4 + k, p * 128 + 124 + k] = 1
            vze[64 + p * 4 + k, p * 128 + k] = 1
    pb = np.zeros((144, 160), np.float32)
    for y in range(144):
        at = y // 2
        pb[y, at] = 1
        for shift, value in ((-1, (-7, 1)), (0, (8, -8)), (1, (-1, 7))):
            if 0 <= at + shift < 72:
                pb[y, 80 + at + shift] = value[y % 2]

    def lane(c, z):
        if z < 0:
            return 384 + c * 8 + z + 8
        if z >= 64:
            return 432 + c * 8 + z - 64
        return c * 64 + z

    q1 = np.zeros((1024, 768), np.float32)
    q2 = np.zeros((512, 768), np.float32)
    for i in range(3):
        cx, cy, cz = pair_table[i]
        for z in range(-2, 130):
            out = i * 256 + (z if 0 <= z < 128 else (128 + z - 128 if z >= 128 else 256 + z))
            at = z // 2
            q1[lane(cx, at), out] = 1
            q2[lane(cy, at), out] = 1
            for shift, value in ((-1, (-7, 1)), (0, (8, -8)), (1, (-1, 7))):
                q1[512 + lane(cz, at + shift), out] = value[z % 2]
    spread = np.zeros((16, 128), np.float32)
    for zi in range(8):
        for c in range(16):
            spread[c, zi * 16 + c] = 1
    return [jnp.asarray(t, BF) for t in (fsel, fedge, fexp, texp, comp, cedge, cexp, vz, vze, pb, q1, q2, spread)]


def mm(a, b):
    return jnp.dot(a, b, preferred_element_type=F32)


def lanes(shape):
    return lax.broadcasted_iota(jnp.int32, shape, len(shape) - 1)


def write_plane(dst, p, value):
    low = lanes((ROWS, 128)) < 64
    dst[p, :, 0:128] = value.astype(BF)
    up = jnp.concatenate([value[RY:], value[:RY]], axis=0)
    down = jnp.concatenate([value[ROWS - RY :], value[: ROWS - RY]], axis=0)
    dst[p, :, 128:256] = jnp.where(low, up, down).astype(BF)


def conv_plane(src, p, kernel):
    lhs = jnp.concatenate([src[p], src[p + 1], src[p + 2]], axis=1)
    r = mm(lhs, kernel)
    return pltpu.roll(r[:, 0:128], 1, 0) + r[:, 128:256] + pltpu.roll(r[:, 256:384], ROWS - 1, 0)


def banded(w_ref, spread, wt):
    group = lanes((16, 128)) // 16

    @pl.loop(0, 7)
    def _(k):
        tile = mm(w_ref[k], spread)
        for dx in range(3):
            for dy in range(3):
                taps = [tile[(9 * dx + 3 * dy + dz) * 16 : (9 * dx + 3 * dy + dz + 1) * 16] for dz in range(3)]
                for slot in range(16):
                    z = -1 if slot == 15 else slot
                    value = jnp.zeros((16, 128), F32)
                    if slot <= 8 or slot == 15:
                        for dz in range(3):
                            value = jnp.where(group == z - (dz - 1), taps[dz], value)
                    wt[k, dx * 256 + slot * 16 : dx * 256 + slot * 16 + 16, dy * 128 : dy * 128 + 128] = value.astype(BF)


def weight_gradient(src, first, cots, gsrc, layer, gtmp):
    rhs = []
    for x in range(2):
        c = cots[x]
        rhs.append(jnp.concatenate([pltpu.roll(c, OWN - 1, 0), c, pltpu.roll(c, 1, 0)], axis=1).astype(BF))
    rhs = jnp.concatenate(rhs, axis=0)
    group = lanes((16, 128)) // 16
    for dx in range(3):
        lhs = jnp.concatenate([src[first + dx, RY : RY + OWN], src[first + dx + 1, RY : RY + OWN]], axis=0)
        gtmp[...] = lax.dot_general(lhs, rhs, (((0,), (0,)), ((), ())), preferred_element_type=F32)
        for dy in range(3):
            for dz in range(3):
                h = jnp.zeros((16, 128), F32)
                for zi in range(8):
                    z = zi + dz - 1
                    slot = 15 if z < 0 else z
                    h = h + jnp.where(group == zi, gtmp[slot * 16 : slot * 16 + 16, dy * 128 : dy * 128 + 128], 0.0)
                for step in (64, 32, 16):
                    h = h + pltpu.roll(h, step, 1)
                tap = 9 * dx + 3 * dy + dz
                old = gsrc[layer * 4 + tap // 8] if tap % 8 else jnp.zeros((16, 128), F32)
                gsrc[layer * 4 + tap // 8] = jnp.where(group == tap % 8, h, old)


def stencil(ref, p, t, r, count, low, force, scale):
    def at(i, dp, dy):
        return ref[i, p + dp, t, pl.ds(8 + r + dy, count), :]

    vel = [at(i, 0, 0) for i in range(3)]
    outs = []
    for i in range(3):
        f = vel[i]
        other = ref[i, p, 1 - t, pl.ds(8 + r, count), :]
        zp1 = pltpu.roll(jnp.where(low[0], other, f), 127, 1)
        zp2 = pltpu.roll(jnp.where(low[1], other, f), 126, 1)
        zm1 = pltpu.roll(jnp.where(low[2], other, f), 1, 1)
        zm2 = pltpu.roll(jnp.where(low[3], other, f), 2, 1)
        xp1, xp2, xm1, xm2 = at(i, 1, 0), at(i, 2, 0), at(i, -1, 0), at(i, -2, 0)
        yp1, yp2, ym1, ym2 = at(i, 0, 1), at(i, 0, 2), at(i, 0, -1), at(i, 0, -2)
        adv = vel[0] * (8.0 * (xp1 - xm1) - (xp2 - xm2))
        adv = adv + vel[1] * (8.0 * (yp1 - ym1) - (yp2 - ym2))
        adv = adv + vel[2] * (8.0 * (zp1 - zm1) - (zp2 - zm2))
        near = (xp1 + xm1) + (yp1 + ym1) + (zp1 + zm1)
        far = (xp2 + xm2) + (yp2 + ym2) + (zp2 + zm2)
        lap = 8.0 * near - 45.0 * f - 0.5 * far
        outs.append(scale * ((lap - adv) * (1.0 / 12.0) + force(i)))
    return vel, outs


def body(
    v, w7, fsel, fedge, fexp, texp, comp, cedge, cexp, vz, vze, pb, q1, q2, spread,
    vnext, sw, gout,
    fpx, fe, fer, vb, vbx, vzs, vzr, vzf, tx, wt, xe0, xe1, xe2, xe3, c4, xe4, xc3, xc2, xc1, mask,
    cpx, spx, ce, cer, se, ser, gxt, r2s, force, vext, fs, gtmp, gsrc, r1, r2g, ssem, rsem,
):
    g = lax.axis_index("grp")
    s = lax.axis_index("slab")
    used = [0]
    sent = []

    def slab_at(k):
        return {"slab": lax.rem(s + (k + SLAB), SLAB)}

    def grp_at(k):
        return {"grp": lax.rem(g + (k + GRP), GRP)}

    def send(src, dst, device):
        k = used[0]
        used[0] += 1
        copy = pltpu.make_async_remote_copy(
            src_ref=src, dst_ref=dst, send_sem=ssem.at[k], recv_sem=rsem.at[k], device_id=device, device_id_type=MESH
        )
        copy.start()
        sent.append(copy)
        return copy

    quad = lax.rem(s, 4)
    a = g * 4 + quad
    b = s // 4

    def peer_a(k):
        other = lax.rem(a + k, 16)
        return other, {"grp": other // 4, "slab": b * 4 + lax.rem(other, 4)}

    def peer_b(k):
        return {"slab": lax.rem(b + k, 8) * 4 + quad}

    barrier = pltpu.get_barrier_semaphore()
    friends = [slab_at(k) for k in (-3, -2, -1, 1, 2, 3)]
    friends += [peer_a(k)[1] for k in range(1, 16)] + [peer_b(k) for k in range(1, 8)]
    for friend in friends:
        pl.semaphore_signal(barrier, inc=1, device_id=friend, device_id_type=MESH)
    pl.semaphore_wait(barrier, len(friends))

    for X in range(2):
        fine = [[v[c, 2 * X + px, pl.ds(py, 72, stride=2), :] for px in range(2) for py in range(2)] for c in range(3)]

        def mean(parts):
            total = (parts[0] + parts[1]) + (parts[2] + parts[3])
            return (total + pltpu.roll(total, 127, 1)) * 0.125

        means = [mean(fine[c]) for c in range(3)]
        blank = jnp.zeros((8, 128), F32)
        fields = [jnp.concatenate([m, blank], axis=0).astype(BF) for m in means]
        targets = []
        for i, j in stress_pairs:
            t = mean([fine[i][n] * fine[j][n] for n in range(4)]) - means[i] * means[j]
            targets.append(jnp.concatenate([t, blank], axis=0).astype(BF))
        fpx[5 + X, :, 0:128] = mm(jnp.concatenate(fields[:2], axis=1), fsel[...]).astype(BF)
        fpx[5 + X, :, 128:256] = mm(fields[2], fsel[0:128]).astype(BF)
        joined = jnp.concatenate(fields, axis=1)
        for side in range(2):
            fe[side, X] = mm(joined, fedge[side]).astype(BF)
        t = mm(jnp.concatenate(targets, axis=1), texp[...])
        for zb in range(8):
            tx[X, zb * RY : zb * RY + RY] = t[:, zb * 128 : zb * 128 + 128]
    vb[...] = v[...].astype(BF)
    joined = jnp.concatenate([vb[c, x] for c in range(3) for x in range(4)], axis=1)
    for side in range(2):
        vzs[side] = mm(joined, vz[side]).astype(BF)

    zc = []
    for side, k in ((0, 1), (1, -1)):
        zc.append(send(fe.at[side], fer.at[side], grp_at(k)))
        zc.append(send(vzs.at[side], vzr.at[side], grp_at(k)))
    for copy in zc:
        copy.wait_recv()
    for X in range(2):
        fpx[5 + X, :, 128:256] = fpx[5 + X, :, 128:256] + fer[0, X] + fer[1, X]
    vzf[1] = vzr[0] + vzr[1]
    fc = []
    fc.append(send(fpx.at[pl.ds(5, 2)], fpx.at[pl.ds(3, 2)], slab_at(1)))
    fc.append(send(fpx.at[pl.ds(5, 2)], fpx.at[pl.ds(7, 2)], slab_at(-1)))
    fc.append(send(fpx.at[pl.ds(5, 2)], fpx.at[pl.ds(1, 2)], slab_at(2)))
    fc.append(send(fpx.at[pl.ds(5, 2)], fpx.at[pl.ds(9, 2)], slab_at(-2)))
    fc.append(send(fpx.at[pl.ds(6, 1)], fpx.at[pl.ds(0, 1)], slab_at(3)))
    fc.append(send(fpx.at[pl.ds(5, 1)], fpx.at[pl.ds(11, 1)], slab_at(-3)))
    vc = []
    for place, k in ((0, 1), (1, -1)):
        vc.append(send(vb, vbx.at[place], slab_at(k)))
        vc.append(send(vzf.at[1], vzf.at[2 * place], slab_at(k)))

    banded(w7, spread[...], wt)
    for zb in range(NB):
        mask[zb * RY : zb * RY + 72] = jnp.ones((72, 128), F32)
        mask[zb * RY + 72 : zb * RY + RY] = jnp.zeros((8, 128), F32)
    for copy in fc:
        copy.wait_recv()

    def expand(src, table, dst, count):
        @pl.loop(0, count)
        def _(p):
            r = mm(src[p], table[...])
            write_plane(dst, p, jnp.concatenate([r[:, zb * 128 : zb * 128 + 128] for zb in range(NB)], axis=0))

    expand(fpx, fexp, xe0, 12)

    for k, (src, dst, count) in enumerate(((xe0, xe1, 10), (xe1, xe2, 8), (xe2, xe3, 6))):

        @pl.loop(0, count)
        def _(p, src=src, dst=dst, k=k):
            write_plane(dst, p, jnp.tanh(conv_plane(src, p, wt[k])) * mask[...])

    for X in range(2):
        pred = (conv_plane(xe3, X + 1, wt[3]) * mask[...])[RY : RY + OWN]
        stress = pred.astype(BF)
        cot = (2.0 / SIZE * (pred - tx[X])).astype(BF)
        c4[X] = cot.astype(F32)
        for value, pack, edges, at in ((cot, cpx, ce, 3), (stress, spx, se, 2)):
            joined = jnp.concatenate([value[zb * RY : zb * RY + RY] for zb in range(8)], axis=1)
            pack[at + X, :, 0:384] = mm(joined, comp[...]).astype(BF)
            edges[0, X] = mm(value[7 * RY : 8 * RY], cedge[0]).astype(BF)
            edges[1, X] = mm(value[0:RY], cedge[1]).astype(BF)

    zc = []
    for side, k in ((0, 1), (1, -1)):
        zc.append(send(ce.at[side], cer.at[side], grp_at(k)))
        zc.append(send(se.at[side], ser.at[side], grp_at(k)))
    for copy in zc:
        copy.wait_recv()
    for X in range(2):
        cpx[3 + X, :, 384:512] = cer[0, X] + cer[1, X]
        spx[2 + X, :, 384:512] = ser[0, X] + ser[1, X]
    cc = []
    cc.append(send(cpx.at[pl.ds(3, 2)], cpx.at[pl.ds(1, 2)], slab_at(1)))
    cc.append(send(cpx.at[pl.ds(3, 2)], cpx.at[pl.ds(5, 2)], slab_at(-1)))
    cc.append(send(cpx.at[pl.ds(4, 1)], cpx.at[pl.ds(0, 1)], slab_at(2)))
    cc.append(send(cpx.at[pl.ds(3, 1)], cpx.at[pl.ds(7, 1)], slab_at(-2)))
    sc = []
    sc.append(send(spx.at[pl.ds(2, 2)], spx.at[pl.ds(0, 2)], slab_at(1)))
    sc.append(send(spx.at[pl.ds(2, 2)], spx.at[pl.ds(4, 2)], slab_at(-1)))
    wc = []
    for k in range(1, GRP):
        other = lax.rem(g + k, GRP)
        rows = pl.ds(pl.multiple_of(other * 16, 16), 32)
        wc.append(send(spx.at[pl.ds(2, 2), rows, pl.ds(0, 384)], sw.at[g], grp_at(k)))
    rows = pl.ds(pl.multiple_of(g * 16, 16), 32)
    sw[g] = spx[2:4, rows, 0:384]

    weight_gradient(xe3, 1, [c4[0], c4[1]], gsrc, 3, gtmp)

    for copy in vc:
        copy.wait_recv()
    pads = jnp.zeros((8, 128), F32)
    for c in range(3):

        @pl.loop(0, 12)
        def _(p, c=c):
            for t in range(2):
                vext[c, p, t, 0:8] = pads
                vext[c, p, t, 152:160] = pads

        @pl.loop(0, 8)
        def _(p, c=c):
            for t in range(2):
                fs[c, p, t, 0:8] = pads
                fs[c, p, t, 152:160] = pads

        for x in range(4):
            vext[c, x, 0, 8:152] = vbx[0, c, x].astype(F32)
            vext[c, 4 + x, 0, 8:152] = v[c, x]
            vext[c, 8 + x, 0, 8:152] = vbx[1, c, x].astype(F32)
    for n in range(3):
        r = mm(vzf[n], vze[...])
        for c in range(3):
            for x in range(4):
                p = c * 4 + x
                vext[c, 4 * n + x, 1, 8:152] = r[:, p * 128 : p * 128 + 128]

    for copy in cc:
        copy.wait_recv()
    expand(cpx, cexp, xe4, 8)

    def back(src, k, act, shift, dst, count):
        @pl.loop(0, count)
        def _(p):
            below = act[p + shift, :, 0:128].astype(F32)
            write_plane(dst, p, conv_plane(src, p, wt[k]) * (1.0 - below * below) * mask[...])

    def own(ref, at):
        return [ref[at + X, RY : RY + OWN, 0:128].astype(F32) for X in range(2)]

    back(xe4, 4, xe3, 0, xc3, 6)
    weight_gradient(xe2, 2, own(xc3, 2), gsrc, 2, gtmp)
    back(xc3, 5, xe2, 2, xc2, 4)
    weight_gradient(xe1, 3, own(xc2, 1), gsrc, 1, gtmp)
    back(xc2, 6, xe1, 4, xc1, 2)
    weight_gradient(xe0, 4, own(xc1, 0), gsrc, 0, gtmp)

    first = [send(gsrc.at[peer_a(k)[0]], r1.at[k - 1], peer_a(k)[1]) for k in range(1, 16)]

    for copy in sc:
        copy.wait_recv()
    for n in range(8):
        at = 1 + n // 2
        lower, mid, upper = (spx[at + d].astype(F32) for d in (-1, 0, 1))
        if n % 2 == 0:
            slope = 8.0 * mid - upper - 7.0 * lower
        else:
            slope = 7.0 * upper - 8.0 * mid + lower
        gxt[n * RY : n * RY + RY, 0:512] = slope.astype(BF)
        gxt[n * RY : n * RY + RY, 512:1024] = spx[at]
        if n % 2 == 0:
            r2s[n // 2] = mm(spx[at], q2[...]).astype(BF)
    r = mm(gxt[...], q1[...]).astype(BF)
    for n in range(8):
        both = jnp.concatenate([r[n * RY : n * RY + RY], r2s[n // 2]], axis=0)
        force[n] = mm(pb[...], both) * (-4.0 / 12.0)

    for copy in first:
        copy.wait_recv()
    total = gsrc[a]
    for k in range(15):
        total = total + r1[k]
    r2g[b] = total
    second = [send(r2g.at[b], r2g.at[b], peer_b(k)) for k in range(1, 8)]

    count = 48
    lane = lanes((count, 128))
    low = (lane < 1, lane < 2, lane >= 127, lane >= 126)

    @pl.loop(0, 8)
    def _(p):
        for t in range(2):
            for r in range(0, 144, count):
                vel, outs = stencil(
                    vext, p + 2, t, r, count, low,
                    lambda i: force[p, r : r + count, i * 256 + t * 128 : i * 256 + t * 128 + 128], 0.1,
                )
                for i in range(3):
                    fs[i, p, t, 8 + r : 8 + r + count] = vel[i] + outs[i]

    for copy in second:
        copy.wait_recv()
    total = r2g[0]
    for k in range(1, 8):
        total = total + r2g[k]
    gout[a] = total
    third = [send(gout.at[a], gout.at[a], peer_a(k)[1]) for k in range(1, 16)]

    @pl.loop(0, 4)
    def _(x):
        for r in range(0, 144, count):
            vel, outs = stencil(
                fs, x + 2, 0, r, count, low,
                lambda i: force[x + 2, r : r + count, i * 256 : i * 256 + 128], 0.1,
            )
            for i in range(3):
                vnext[i, x, r : r + count] = 0.5 * (v[i, x, r : r + count] + vel[i] + outs[i])

    for copy in third:
        copy.wait_recv()
    for copy in wc:
        copy.wait_recv()
    for copy in sent:
        copy.wait_send()


def forward_rows(weight):
    padded = jnp.pad(weight, ((0, 0), (0, 16 - weight.shape[1]), (0, 16 - weight.shape[2])))
    return jnp.transpose(padded, (0, 2, 1)).reshape(432, 16)


def backward_rows(weight):
    padded = jnp.pad(weight, ((0, 0), (0, 16 - weight.shape[1]), (0, 16 - weight.shape[2])))
    return padded[::-1].reshape(432, 16)


def local(velocity, w_in, w_mid_a, w_mid_b, w_out):
    w7 = jnp.stack(
        [forward_rows(w) for w in (w_in, w_mid_a, w_mid_b, w_out)]
        + [backward_rows(w) for w in (w_out, w_mid_b, w_mid_a)]
    )
    vm = pltpu.VMEM
    scratch = [
        vm((12, RY, 256), BF), vm((2, 2, RY, 128), BF), vm((2, 2, RY, 128), BF),
        vm((3, 4, 144, 128), BF), vm((2, 3, 4, 144, 128), BF),
        vm((2, 144, 128), BF), vm((2, 144, 128), BF), vm((3, 144, 128), BF),
        vm((2, OWN, 128), F32), vm((7, 768, 384), BF),
        vm((12, ROWS, 256), BF), vm((10, ROWS, 256), BF), vm((8, ROWS, 256), BF), vm((6, ROWS, 256), BF),
        vm((2, OWN, 128), F32),
        vm((8, ROWS, 256), BF), vm((6, ROWS, 256), BF), vm((4, ROWS, 256), BF), vm((2, ROWS, 256), BF),
        vm((ROWS, 128), F32),
        vm((8, RY, 512), BF), vm((6, RY, 512), BF),
        vm((2, 2, RY, 128), BF), vm((2, 2, RY, 128), BF), vm((2, 2, RY, 128), BF), vm((2, 2, RY, 128), BF),
        vm((8 * RY, 1024), BF), vm((4, RY, 768), BF), vm((8, 144, 768), F32),
        vm((3, 12, 2, 160, 128), F32), vm((3, 8, 2, 160, 128), F32),
        vm((256, 384), F32), vm((16, 16, 128), F32), vm((15, 16, 128), F32), vm((8, 16, 128), F32),
        pltpu.SemaphoreType.DMA((64,)), pltpu.SemaphoreType.DMA((64,)),
    ]
    consts = tables()
    vnext, sw, gout = pl.pallas_call(
        body,
        out_shape=[
            jax.ShapeDtypeStruct((3, 4, 144, 128), F32),
            jax.ShapeDtypeStruct((4, 2, 32, 384), BF),
            jax.ShapeDtypeStruct((16, 16, 128), F32),
        ],
        in_specs=[pl.BlockSpec(memory_space=pltpu.VMEM)] * (2 + len(consts)),
        out_specs=[pl.BlockSpec(memory_space=pltpu.VMEM)] * 3,
        scratch_shapes=scratch,
        compiler_params=pltpu.CompilerParams(
            collective_id=0, has_side_effects=True, vmem_limit_bytes=62 * 1024 * 1024
        ),
    )(velocity, w7, *consts)
    g = lax.axis_index("grp")
    window = lax.dynamic_slice_in_dim(sw, 2 * g, 18, axis=2).reshape(4, 2, 18, 6, 64)
    stress = jnp.transpose(window, (3, 1, 2, 0, 4)).reshape(6, 2, 18, 256)
    grads = jnp.transpose(gout.reshape(4, 4, 16, 8, 16), (0, 1, 3, 4, 2)).reshape(4, 32, 16, 16)
    return (
        vnext, stress,
        grads[0, :27, :, :3], grads[1, :27], grads[2, :27], grads[3, :27, :6],
    )


def solution(mesh):
    in_specs = (P(None, "slab", None, "grp"), P(), P(), P(), P())
    out_specs = (P(None, "slab", None, "grp"), P(None, "slab", "grp", None), P(), P(), P(), P())
    return jax.shard_map(local, mesh=mesh, in_specs=in_specs, out_specs=out_specs, check_vma=False)
```

```python
import jax
import jax.numpy as jnp
import numpy as np
from jax import lax
from jax.experimental import pallas as pl
from jax.experimental.pallas import tpu as pltpu
from jax.sharding import PartitionSpec as P

MESH = pl.DeviceIdType.MESH
F32 = jnp.float32
BF = jnp.bfloat16
GRP, SLAB = 4, 32
RY = 80
NB = 10
ROWS = NB * RY
OWN = 8 * RY
pair_table = ((0, 3, 4), (3, 1, 5), (4, 5, 2))
stress_pairs = ((0, 0), (1, 1), (2, 2), (0, 1), (0, 2), (1, 2))
SIZE = 6 * 64 * 72 * 256


def tables():
    fsel = np.zeros((256, 128), np.float32)
    for z in range(64):
        fsel[2 * z, z] = 1
        fsel[128 + 2 * z, 64 + z] = 1
    fedge = np.zeros((2, 384, 128), np.float32)
    fexp = np.zeros((256, NB * 128), np.float32)
    for f in range(3):
        for zi in range(8):
            fedge[0, f * 128 + 2 * (56 + zi), 64 + f * 8 + zi] = 1
            fedge[1, f * 128 + 2 * zi, 88 + f * 8 + zi] = 1
        for block in range(NB):
            for kz in range(10):
                z = block * 8 - 9 + kz
                if -8 <= z < 72:
                    at = f * 64 + z if 0 <= z < 64 else (200 + f * 8 + z if z < 0 else 152 + f * 8 + z)
                    fexp[at, block * 128 + kz * 4 + f] = 1
    texp = np.zeros((768, 1024), np.float32)
    comp = np.zeros((1024, 384), np.float32)
    cedge = np.zeros((2, 128, 128), np.float32)
    cexp = np.zeros((512, NB * 128), np.float32)
    for c in range(6):
        for zi in range(8):
            cedge[0, zi * 16 + c, c * 8 + zi] = 1
            cedge[1, zi * 16 + c, 48 + c * 8 + zi] = 1
            for zb in range(8):
                z = zb * 8 + zi
                texp[c * 128 + 2 * z, zb * 128 + zi * 16 + c] = 1
                comp[zb * 128 + zi * 16 + c, c * 64 + z] = 1
        for block in range(NB):
            for kz in range(10):
                z = block * 8 - 9 + kz
                if -8 <= z < 72:
                    at = c * 64 + z if 0 <= z < 64 else (392 + c * 8 + z if z < 0 else 368 + c * 8 + z)
                    cexp[at, block * 128 + kz * 6 + c] = 1
    vz = np.zeros((2, 1536, 128), np.float32)
    vze = np.zeros((128, 1536), np.float32)
    for p in range(12):
        for k in range(4):
            vz[0, p * 128 + 124 + k, p * 4 + k] = 1
            vz[1, p * 128 + k, 64 + p * 4 + k] = 1
            vze[p * 4 + k, p * 128 + 124 + k] = 1
            vze[64 + p * 4 + k, p * 128 + k] = 1
    pb = np.zeros((144, 160), np.float32)
    for y in range(144):
        at = y // 2
        pb[y, at] = 1
        for shift, value in ((-1, (-7, 1)), (0, (8, -8)), (1, (-1, 7))):
            if 0 <= at + shift < 72:
                pb[y, 80 + at + shift] = value[y % 2]

    def lane(c, z):
        if z < 0:
            return 384 + c * 8 + z + 8
        if z >= 64:
            return 432 + c * 8 + z - 64
        return c * 64 + z

    q1 = np.zeros((1024, 768), np.float32)
    q2 = np.zeros((512, 768), np.float32)
    for i in range(3):
        cx, cy, cz = pair_table[i]
        for z in range(-2, 130):
            out = i * 256 + (z if 0 <= z < 128 else (128 + z - 128 if z >= 128 else 256 + z))
            at = z // 2
            q1[lane(cx, at), out] = 1
            q2[lane(cy, at), out] = 1
            for shift, value in ((-1, (-7, 1)), (0, (8, -8)), (1, (-1, 7))):
                q1[512 + lane(cz, at + shift), out] = value[z % 2]
    spread = np.zeros((16, 128), np.float32)
    for zi in range(8):
        for c in range(16):
            spread[c, zi * 16 + c] = 1
    return [jnp.asarray(t, BF) for t in (fsel, fedge, fexp, texp, comp, cedge, cexp, vz, vze, pb, q1, q2, spread)]


def mm(a, b):
    return jnp.dot(a, b, preferred_element_type=F32)


def lanes(shape):
    return lax.broadcasted_iota(jnp.int32, shape, len(shape) - 1)


def edge_group(dx, z):
    return (7, 1, 3)[dx] if z < 0 else (0, 2, 4)[dx]


def row_of(dx, z):
    return dx * 128 + z * 16 if 0 <= z < 8 else 384 + edge_group(dx, z) * 16


def write_plane(dst, p, value):
    lane = lanes((ROWS, 128))
    dst[p, :, 0:128] = value.astype(BF)
    up = jnp.concatenate([value[RY:], value[:RY]], axis=0)
    down = jnp.concatenate([value[ROWS - RY :], value[: ROWS - RY]], axis=0)
    edge = jnp.where(lane < 16, up, jnp.where(lane >= 112, down, 0.0))
    dst[p, :, 128:256] = edge.astype(BF)
    dst[p, :, 256:384] = pltpu.roll(edge, 32, 1).astype(BF)
    dst[p, :, 384:512] = pltpu.roll(edge, 64, 1).astype(BF)


def window(src, p, rows):
    edges = src[p, rows, 128:256] + src[p + 1, rows, 256:384] + src[p + 2, rows, 384:512]
    return jnp.concatenate([src[p, rows, 0:128], src[p + 1, rows, 0:128], src[p + 2, rows, 0:128], edges], axis=1)


def window_fields(src, p, rows):
    return src[p, rows, 0:128] + src[p + 1, rows, 128:256] + src[p + 2, rows, 256:384]


def window_cot(src, p, rows):
    low, mid, high = (lax.rem(p + 8 + k, 12) for k in range(3))
    return jnp.concatenate([src[low, rows, 0:128] + src[mid, rows, 128:256], src[high, rows, 0:128]], axis=1)


def conv_plane(lhs, kernel):
    r = mm(lhs, kernel)
    return pltpu.roll(r[:, 0:128], 1, 0) + r[:, 128:256] + pltpu.roll(r[:, 256:384], ROWS - 1, 0)


ALL = slice(0, ROWS)
MID = slice(RY, RY + OWN)


def banded(w_in, w_a, w_b, w_out, spread, wt, w1, w4, wf, tiles):
    group = lanes((16, 128)) // 16

    def turned(w, tap):
        return lax.dot_general(w[tap], spread[0 : w.shape[1]], (((0,), (0,)), ((), ())), preferred_element_type=F32)

    def fill(out):
        for dx in range(3):
            for dy in range(3):
                at = slice(dy * 128, dy * 128 + 128)
                for z in range(-1, 9):
                    value = jnp.zeros((16, 128), F32)
                    for dz in range(3):
                        value = jnp.where(group == z - (dz - 1), tiles[9 * dx + 3 * dy + dz], value)
                    row = row_of(dx, z)
                    wt[out, row : row + 16, at] = value.astype(BF)
        wt[out, 464:496] = jnp.zeros((32, 384), BF)

    for out, w in enumerate((w_a, w_b, w_out)):
        for tap in range(27):
            tiles[tap] = turned(w, tap)
        fill(out)
    for out, w in ((3, w_b), (4, w_a)):
        for tap in range(27):
            tiles[tap] = mm(w[26 - tap], spread)
        fill(out)

    def small(count, starts):
        wf[...] = jnp.zeros((256, 384), F32)
        part = lanes((count, 128)) // 16
        for dx in range(3):
            for dy in range(3):
                for kz in range(10):
                    value = jnp.zeros((count, 128), F32)
                    for dz in range(3):
                        value = jnp.where(part == kz - dz, tiles[9 * dx + 3 * dy + dz, 0:count], value)
                    row = starts[dx] + kz * count
                    wf[row : row + count, dy * 128 : dy * 128 + 128] = value

    for tap in range(27):
        tiles[tap, 0:3] = turned(w_in, tap)
        tiles[tap, 3:4] = jnp.zeros((1, 128), F32)
    small(4, (0, 40, 80))
    w1[...] = wf[0:128].astype(BF)
    for tap in range(27):
        tiles[tap, 0:6] = mm(w_out[26 - tap], spread)
    small(6, (0, 60, 128))
    w4[...] = wf[...].astype(BF)


def shifted_cots(cots):
    both = [
        jnp.concatenate([pltpu.roll(c, OWN - 1, 0), c, pltpu.roll(c, 1, 0)], axis=1).astype(BF) for c in cots
    ]
    return jnp.concatenate(both, axis=0)


def keep_tap(gsrc, layer, tap, h):
    group = lanes((16, 128)) // 16
    old = gsrc[layer * 4 + tap // 8] if tap % 8 else jnp.zeros((16, 128), F32)
    gsrc[layer * 4 + tap // 8] = jnp.where(group == tap % 8, h, old)


def weight_gradient(src, first, cots, gsrc, layer, gtmp):
    rhs = jnp.concatenate([window(src, first + x, MID) for x in range(2)], axis=0)
    gtmp[...] = lax.dot_general(shifted_cots(cots), rhs, (((0,), (0,)), ((), ())), preferred_element_type=F32)
    group = lanes((16, 128)) // 16
    for dx in range(3):
        for dy in range(3):
            for dz in range(3):
                h = jnp.zeros((16, 128), F32)
                extra = None
                for zi in range(8):
                    z = zi + dz - 1
                    row = slice(dy * 128 + zi * 16, dy * 128 + zi * 16 + 16)
                    if 0 <= z < 8:
                        h = jnp.where(group == z, gtmp[row, dx * 128 : dx * 128 + 128], h)
                    else:
                        extra = jnp.where(group == edge_group(dx, z), gtmp[row, 384:512], 0.0)
                if extra is not None:
                    h = h + extra
                for step in (64, 32, 16):
                    h = h + pltpu.roll(h, step, 1)
                keep_tap(gsrc, layer, 9 * dx + 3 * dy + dz, h)


def first_gradient(src, first, cots, gsrc, gtmp):
    rhs = jnp.concatenate([window_fields(src, first + x, MID) for x in range(2)], axis=0)
    gtmp[:, 0:128] = lax.dot_general(shifted_cots(cots), rhs, (((0,), (0,)), ((), ())), preferred_element_type=F32)
    part = lanes((16, 128)) // 4
    for dx in range(3):
        for dy in range(3):
            for dz in range(3):
                h = jnp.zeros((16, 128), F32)
                for zi in range(8):
                    row = slice(dy * 128 + zi * 16, dy * 128 + zi * 16 + 16)
                    h = jnp.where(part == dx * 10 + zi + dz, gtmp[row, 0:128], h)
                for step in (112, 120, 124):
                    h = h + pltpu.roll(h, step, 1)
                tap = 9 * dx + 3 * dy + dz
                turn = ((tap % 8) * 16 - (dx * 40 + dz * 4)) % 128
                keep_tap(gsrc, 0, tap, pltpu.roll(h, turn, 1) if turn else h)


def stencil(ref, p, t, r, count, low):
    def at(i, dp, dy):
        return ref[i, p + dp, t, pl.ds(8 + r + dy, count), :]

    vel = [at(i, 0, 0) for i in range(3)]
    outs = []
    for i in range(3):
        f = vel[i]
        other = ref[i, p, 1 - t, pl.ds(8 + r, count), :]
        zp1 = pltpu.roll(jnp.where(low[0], other, f), 127, 1)
        zp2 = pltpu.roll(jnp.where(low[1], other, f), 126, 1)
        zm1 = pltpu.roll(jnp.where(low[2], other, f), 1, 1)
        zm2 = pltpu.roll(jnp.where(low[3], other, f), 2, 1)
        xp1, xp2, xm1, xm2 = at(i, 1, 0), at(i, 2, 0), at(i, -1, 0), at(i, -2, 0)
        yp1, yp2, ym1, ym2 = at(i, 0, 1), at(i, 0, 2), at(i, 0, -1), at(i, 0, -2)
        adv = vel[0] * (8.0 * (xp1 - xm1) - (xp2 - xm2))
        adv = adv + vel[1] * (8.0 * (yp1 - ym1) - (yp2 - ym2))
        adv = adv + vel[2] * (8.0 * (zp1 - zm1) - (zp2 - zm2))
        near = (xp1 + xm1) + (yp1 + ym1) + (zp1 + zm1)
        far = (xp2 + xm2) + (yp2 + ym2) + (zp2 + zm2)
        lap = 8.0 * near - 45.0 * f - 0.5 * far
        outs.append((lap - adv) * (0.1 / 12.0))
    return vel, outs


def body(
    v, w_in, w_a, w_b, w_out, spread, *refs
):
    far = refs[:12]
    vnext, sw, gout = refs[12:15]
    near = refs[15:27]
    fsel, fedge, fexp, texp, comp, cedge, cexp, vz, vze, pb, q1, q2 = near
    (
        fpx, fe, fer, vb, vbx, vzs, vzr, vzf, tx, wt, w1, w4, wf, tiles, xe0, xe1, xe2, xe3, c4, c1, mask,
        cpx, spx, ce, cer, se, ser, gxt, r2s, force, vext, fs, gtmp, gsrc, r1, r2g, csem, ssem, rsem,
    ) = refs[27:]
    held = [pltpu.make_async_copy(far[n], near[n], csem.at[n]) for n in range(12)]
    for copy in held:
        copy.start()
    g = lax.axis_index("grp")
    s = lax.axis_index("slab")
    used = [0]
    sent = []

    def slab_at(k):
        return {"slab": lax.rem(s + (k + SLAB), SLAB)}

    def grp_at(k):
        return {"grp": lax.rem(g + (k + GRP), GRP)}

    def send(src, dst, device):
        k = used[0]
        used[0] += 1
        copy = pltpu.make_async_remote_copy(
            src_ref=src, dst_ref=dst, send_sem=ssem.at[k], recv_sem=rsem.at[k], device_id=device, device_id_type=MESH
        )
        copy.start()
        sent.append(copy)
        return copy

    quad = lax.rem(s, 4)
    a = g * 4 + quad
    b = s // 4

    def peer_a(k):
        other = lax.rem(a + k, 16)
        return other, {"grp": other // 4, "slab": b * 4 + lax.rem(other, 4)}

    def peer_b(k):
        return {"slab": lax.rem(b + k, 8) * 4 + quad}

    barrier = pltpu.get_barrier_semaphore()
    friends = [slab_at(k) for k in (-3, -2, -1, 1, 2, 3)]
    friends += [peer_a(k)[1] for k in range(1, 16)] + [peer_b(k) for k in range(1, 8)]
    for friend in friends:
        pl.semaphore_signal(barrier, inc=1, device_id=friend, device_id_type=MESH)

    held[0].wait()
    held[1].wait()
    parts = []
    blank = jnp.zeros((8, 128), F32)

    def mean(four):
        total = (four[0] + four[1]) + (four[2] + four[3])
        return (total + pltpu.roll(total, 127, 1)) * 0.125

    for X in range(2):
        fine = [[v[c, 2 * X + px, pl.ds(py, 72, stride=2), :] for px in range(2) for py in range(2)] for c in range(3)]
        means = [mean(fine[c]) for c in range(3)]
        parts.append((fine, means))
        fields = [jnp.concatenate([m, blank], axis=0).astype(BF) for m in means]
        fpx[5 + X, :, 0:128] = mm(jnp.concatenate(fields[:2], axis=1), fsel[...]).astype(BF)
        fpx[5 + X, :, 128:256] = mm(fields[2], fsel[0:128]).astype(BF)
        joined = jnp.concatenate(fields, axis=1)
        for side in range(2):
            fe[side, X] = mm(joined, fedge[side]).astype(BF)
    pl.semaphore_wait(barrier, len(friends))
    zc = [send(fe.at[side], fer.at[side], grp_at(k)) for side, k in ((0, 1), (1, -1))]

    vb[...] = v[...].astype(BF)
    held[7].wait()
    joined = jnp.concatenate([vb[c, x] for c in range(3) for x in range(4)], axis=1)
    for side in range(2):
        vzs[side] = mm(joined, vz[side]).astype(BF)
    uc = [send(vzs.at[side], vzr.at[side], grp_at(k)) for side, k in ((0, 1), (1, -1))]

    for copy in zc:
        copy.wait_recv()
    for X in range(2):
        fpx[5 + X, :, 128:256] = fpx[5 + X, :, 128:256] + fer[0, X] + fer[1, X]
    fc = []
    fc.append(send(fpx.at[pl.ds(5, 2)], fpx.at[pl.ds(3, 2)], slab_at(1)))
    fc.append(send(fpx.at[pl.ds(5, 2)], fpx.at[pl.ds(7, 2)], slab_at(-1)))
    fc.append(send(fpx.at[pl.ds(6, 1)], fpx.at[pl.ds(0, 1)], slab_at(3)))
    fc.append(send(fpx.at[pl.ds(5, 1)], fpx.at[pl.ds(11, 1)], slab_at(-3)))
    fc.append(send(fpx.at[pl.ds(5, 2)], fpx.at[pl.ds(1, 2)], slab_at(2)))
    fc.append(send(fpx.at[pl.ds(5, 2)], fpx.at[pl.ds(9, 2)], slab_at(-2)))

    banded(w_in, w_a, w_b, w_out, spread[...], wt, w1, w4, wf, tiles)
    for zb in range(NB):
        mask[zb * RY : zb * RY + 72] = jnp.ones((72, 128), F32)
        mask[zb * RY + 72 : zb * RY + RY] = jnp.zeros((8, 128), F32)
    held[3].wait()
    for X in range(2):
        fine, means = parts[X]
        targets = []
        for i, j in stress_pairs:
            t = mean([fine[i][n] * fine[j][n] for n in range(4)]) - means[i] * means[j]
            targets.append(jnp.concatenate([t, blank], axis=0).astype(BF))
        t = mm(jnp.concatenate(targets, axis=1), texp[...])
        for zb in range(8):
            tx[X, zb * RY : zb * RY + RY] = t[:, zb * 128 : zb * 128 + 128]
    for copy in uc:
        copy.wait_recv()
    vzf[1] = vzr[0] + vzr[1]
    for copy in fc:
        copy.wait_recv()
    vc = []
    for place, k in ((0, 1), (1, -1)):
        vc.append(send(vb, vbx.at[place], slab_at(k)))
        vc.append(send(vzf.at[1], vzf.at[2 * place], slab_at(k)))

    def expand(src, table, dst, count, shifts, start):
        width = src.shape[2]

        @pl.loop(0, count // 4)
        def _(q):
            r = mm(src[pl.ds(q * 4, 4)].reshape(4 * RY, width), table[...])
            for n in range(4):
                for zb in range(NB):
                    block = r[n * RY : n * RY + RY, zb * 128 : zb * 128 + 128]
                    for m, shift in enumerate(shifts):
                        moved = pltpu.roll(block, shift, 1) if shift else block
                        dst[lax.rem(q * 4 + start, 12) + n, zb * RY : zb * RY + RY, m * 128 : m * 128 + 128] = moved.astype(BF)

    held[2].wait()
    expand(fpx, fexp, xe0, 12, (0, 40, 80), 0)

    @pl.loop(0, 10)
    def _(p):
        write_plane(xe1, p, jnp.tanh(conv_plane(window_fields(xe0, p, ALL), w1[...])) * mask[...])

    for k, (src, dst, count) in enumerate(((xe1, xe2, 8), (xe2, xe3, 6))):

        @pl.loop(0, count)
        def _(p, src=src, dst=dst, k=k):
            write_plane(dst, p, jnp.tanh(conv_plane(window(src, p, ALL), wt[k])) * mask[...])

    held[4].wait()
    held[5].wait()
    for X in range(2):
        pred = (conv_plane(window(xe3, X + 1, ALL), wt[2]) * mask[...])[RY : RY + OWN]
        stress = pred.astype(BF)
        cot = (2.0 / SIZE * (pred - tx[X])).astype(BF)
        c4[X] = cot.astype(F32)
        for value, pack, edges, at in ((cot, cpx, ce, 3), (stress, spx, se, 2)):
            joined = jnp.concatenate([value[zb * RY : zb * RY + RY] for zb in range(8)], axis=1)
            pack[at + X, :, 0:384] = mm(joined, comp[...]).astype(BF)
            edges[0, X] = mm(value[7 * RY : 8 * RY], cedge[0]).astype(BF)
            edges[1, X] = mm(value[0:RY], cedge[1]).astype(BF)

    zc = []
    for side, k in ((0, 1), (1, -1)):
        zc.append(send(ce.at[side], cer.at[side], grp_at(k)))
        zc.append(send(se.at[side], ser.at[side], grp_at(k)))
    for copy in zc:
        copy.wait_recv()
    for X in range(2):
        cpx[3 + X, :, 384:512] = cer[0, X] + cer[1, X]
        spx[2 + X, :, 384:512] = ser[0, X] + ser[1, X]
    cc = []
    cc.append(send(cpx.at[pl.ds(3, 2)], cpx.at[pl.ds(1, 2)], slab_at(1)))
    cc.append(send(cpx.at[pl.ds(3, 2)], cpx.at[pl.ds(5, 2)], slab_at(-1)))
    cc.append(send(cpx.at[pl.ds(4, 1)], cpx.at[pl.ds(0, 1)], slab_at(2)))
    cc.append(send(cpx.at[pl.ds(3, 1)], cpx.at[pl.ds(7, 1)], slab_at(-2)))
    weight_gradient(xe3, 1, [c4[0], c4[1]], gsrc, 3, gtmp)

    for copy in vc:
        copy.wait_recv()
    pads = jnp.zeros((8, 128), F32)
    for c in range(3):

        @pl.loop(0, 12)
        def _(p, c=c):
            for t in range(2):
                vext[c, p, t, 0:8] = pads
                vext[c, p, t, 152:160] = pads

        @pl.loop(0, 8)
        def _(p, c=c):
            for t in range(2):
                fs[c, p, t, 0:8] = pads
                fs[c, p, t, 152:160] = pads

        for x in range(4):
            vext[c, x, 0, 8:152] = vbx[0, c, x].astype(F32)
            vext[c, 4 + x, 0, 8:152] = v[c, x]
            vext[c, 8 + x, 0, 8:152] = vbx[1, c, x].astype(F32)
    held[8].wait()
    for n in range(3):
        r = mm(vzf[n], vze[...])
        for c in range(3):
            for x in range(4):
                p = c * 4 + x
                vext[c, 4 * n + x, 1, 8:152] = r[:, p * 128 : p * 128 + 128]

    count = 48
    lane = lanes((count, 128))
    low = (lane < 1, lane < 2, lane >= 127, lane >= 126)

    @pl.loop(0, 8)
    def _(p):
        for t in range(2):
            for r in range(0, 144, count):
                vel, outs = stencil(vext, p + 2, t, r, count, low)
                for i in range(3):
                    fs[i, p, t, 8 + r : 8 + r + count] = vel[i] + outs[i]

    for copy in cc:
        copy.wait_recv()
    sc = []
    sc.append(send(spx.at[pl.ds(2, 2)], spx.at[pl.ds(0, 2)], slab_at(1)))
    sc.append(send(spx.at[pl.ds(2, 2)], spx.at[pl.ds(4, 2)], slab_at(-1)))
    wc = []
    for k in range(1, GRP):
        other = lax.rem(g + k, GRP)
        rows = pl.ds(pl.multiple_of(other * 16, 16), 32)
        wc.append(send(spx.at[pl.ds(2, 2), rows, pl.ds(0, 384)], sw.at[g], grp_at(k)))
    rows = pl.ds(pl.multiple_of(g * 16, 16), 32)
    sw[g] = spx[2:4, rows, 0:384]

    held[6].wait()
    expand(cpx, cexp, xe0, 8, (0, 60), 8)

    def damp(act, p):
        below = act[p, :, 0:128].astype(F32)
        return (1.0 - below * below) * mask[...]

    @pl.loop(0, 6)
    def _(p):
        write_plane(xe3, p, conv_plane(window_cot(xe0, p, ALL), w4[...]) * damp(xe3, p))

    def own(ref, at):
        return [ref[at + X, MID, 0:128].astype(F32) for X in range(2)]

    weight_gradient(xe2, 2, own(xe3, 2), gsrc, 2, gtmp)

    @pl.loop(0, 4)
    def _(p):
        write_plane(xe2, p + 2, conv_plane(window(xe3, p, ALL), wt[3]) * damp(xe2, p + 2))

    weight_gradient(xe1, 3, own(xe2, 3), gsrc, 1, gtmp)
    for X in range(2):
        c1[X] = (conv_plane(window(xe2, X + 2, ALL), wt[4]) * damp(xe1, X + 4))[MID].astype(BF).astype(F32)
    first_gradient(xe0, 4, [c1[0], c1[1]], gsrc, gtmp)

    first = [send(gsrc.at[peer_a(k)[0]], r1.at[k - 1], peer_a(k)[1]) for k in range(1, 16)]

    for copy in sc:
        copy.wait_recv()
    for n in (9, 10, 11):
        held[n].wait()
    for n in range(8):
        at = 1 + n // 2
        lower, mid, upper = (spx[at + d].astype(F32) for d in (-1, 0, 1))
        if n % 2 == 0:
            slope = 8.0 * mid - upper - 7.0 * lower
        else:
            slope = 7.0 * upper - 8.0 * mid + lower
        gxt[n * RY : n * RY + RY, 0:512] = slope.astype(BF)
        gxt[n * RY : n * RY + RY, 512:1024] = spx[at]
        if n % 2 == 0:
            r2s[n // 2] = mm(spx[at], q2[...]).astype(BF)
    r = mm(gxt[...], q1[...]).astype(BF)
    for n in range(8):
        both = jnp.concatenate([r[n * RY : n * RY + RY], r2s[n // 2]], axis=0)
        force[n] = mm(pb[...], both) * (-4.0 / 12.0)

    for copy in first:
        copy.wait_recv()
    total = gsrc[a]
    for k in range(15):
        total = total + r1[k]
    r2g[b] = total
    second = [send(r2g.at[b], r2g.at[b], peer_b(k)) for k in range(1, 8)]

    @pl.loop(0, 8)
    def _(p):
        for t in range(2):
            for i in range(3):
                at = i * 256 + t * 128
                fs[i, p, t, 8:152] = fs[i, p, t, 8:152] + 0.1 * force[p, :, at : at + 128]

    for copy in second:
        copy.wait_recv()
    total = r2g[0]
    for k in range(1, 8):
        total = total + r2g[k]
    gout[a] = total
    third = [send(gout.at[a], gout.at[a], peer_a(k)[1]) for k in range(1, 16)]

    @pl.loop(0, 4)
    def _(x):
        for r in range(0, 144, count):
            vel, outs = stencil(fs, x + 2, 0, r, count, low)
            for i in range(3):
                again = outs[i] + 0.1 * force[x + 2, r : r + count, i * 256 : i * 256 + 128]
                vnext[i, x, r : r + count] = 0.5 * (v[i, x, r : r + count] + vel[i] + again)

    for copy in third:
        copy.wait_recv()
    for copy in wc:
        copy.wait_recv()
    for copy in sent:
        copy.wait_send()


def finish(vnext, sw, gout, vout, stress, g0, g1, g2, g3, rows):
    vout[...] = vnext[...]
    start = 2 * lax.axis_index("grp")
    low = lanes((18, 128)) < 64
    for tile in range(3):
        rows[tile] = sw[:, :, :, tile * 128 : tile * 128 + 128].astype(F32)
    for x in range(2):
        for c in range(6):
            for half in range(2):
                left = rows[c // 2, 2 * half, x, pl.ds(start, 18), :]
                right = rows[c // 2, 2 * half + 1, x, pl.ds(start, 18), :]
                if c % 2:
                    left = pltpu.roll(left, 64, 1)
                else:
                    right = pltpu.roll(right, 64, 1)
                stress[c, x, :, half * 128 : half * 128 + 128] = jnp.where(low, left, right).astype(BF)
    for layer, out in enumerate((g0, g1, g2, g3)):
        for tap in range(27):
            at = tap % 8 * 16
            out[tap] = gout[layer * 4 + tap // 8, 0 : out.shape[1], at : at + out.shape[2]]


def local(velocity, w_in, w_mid_a, w_mid_b, w_out):
    vm = pltpu.VMEM
    scratch = [
        vm((12, RY, 256), BF), vm((2, 2, RY, 128), BF), vm((2, 2, RY, 128), BF),
        vm((3, 4, 144, 128), BF), vm((2, 3, 4, 144, 128), BF),
        vm((2, 144, 128), BF), vm((2, 144, 128), BF), vm((3, 144, 128), BF),
        vm((2, OWN, 128), F32), vm((5, 512, 384), BF),
        vm((128, 384), BF), vm((256, 384), BF), vm((256, 384), F32), vm((27, 16, 128), F32),
        vm((12, ROWS, 384), BF), vm((10, ROWS, 512), BF), vm((8, ROWS, 512), BF), vm((6, ROWS, 512), BF),
        vm((2, OWN, 128), F32),
        vm((2, OWN, 128), F32),
        vm((ROWS, 128), F32),
        vm((8, RY, 512), BF), vm((6, RY, 512), BF),
        vm((2, 2, RY, 128), BF), vm((2, 2, RY, 128), BF), vm((2, 2, RY, 128), BF), vm((2, 2, RY, 128), BF),
        vm((8 * RY, 1024), BF), vm((4, RY, 768), BF), vm((8, 144, 768), F32),
        vm((3, 12, 2, 160, 128), F32), vm((3, 8, 2, 160, 128), F32),
        vm((384, 512), F32), vm((16, 16, 128), F32), vm((15, 16, 128), F32), vm((8, 16, 128), F32),
        pltpu.SemaphoreType.DMA((12,)), pltpu.SemaphoreType.DMA((64,)), pltpu.SemaphoreType.DMA((64,)),
    ]
    *consts, spread = tables()
    scratch = [vm(t.shape, BF) for t in consts] + scratch
    inside = pl.BlockSpec(memory_space=pltpu.VMEM)
    vnext, sw, gout = pl.pallas_call(
        body,
        out_shape=[
            jax.ShapeDtypeStruct((3, 4, 144, 128), F32),
            jax.ShapeDtypeStruct((4, 2, 32, 384), BF),
            jax.ShapeDtypeStruct((16, 16, 128), F32),
        ],
        in_specs=[inside] * 6 + [pl.BlockSpec(memory_space=pl.ANY)] * len(consts),
        out_specs=[inside] * 3,
        scratch_shapes=scratch,
        compiler_params=pltpu.CompilerParams(
            collective_id=0, has_side_effects=True, vmem_limit_bytes=62 * 1024 * 1024
        ),
    )(velocity, w_in, w_mid_a, w_mid_b, w_out, spread, *consts)
    shapes = [((3, 4, 144, 128), F32), ((6, 2, 18, 256), BF)]
    shapes += [((27, 16, 3), F32), ((27, 16, 16), F32), ((27, 16, 16), F32), ((27, 6, 16), F32)]
    return tuple(
        pl.pallas_call(
            finish,
            out_shape=[jax.ShapeDtypeStruct(*shape) for shape in shapes],
            in_specs=[inside] * 3,
            out_specs=[inside] * 6,
            scratch_shapes=[vm((3, 4, 2, 32, 128), F32)],
            compiler_params=pltpu.CompilerParams(vmem_limit_bytes=32 * 1024 * 1024),
        )(vnext, sw, gout)
    )


def solution(mesh):
    in_specs = (P(None, "slab", None, "grp"), P(), P(), P(), P())
    out_specs = (P(None, "slab", None, "grp"), P(None, "slab", "grp", None), P(), P(), P(), P())
    return jax.shard_map(local, mesh=mesh, in_specs=in_specs, out_specs=out_specs, check_vma=False)
```

```python
import jax
import jax.numpy as jnp
import numpy as np
from jax import lax
from jax.experimental import pallas as pl
from jax.experimental.pallas import tpu as pltpu
from jax.sharding import PartitionSpec as P

MESH = pl.DeviceIdType.MESH
F32 = jnp.float32
BF = jnp.bfloat16
GRP, SLAB = 4, 32
RY = 80
NB = 10
ROWS = NB * RY
OWN = 8 * RY
pair_table = ((0, 3, 4), (3, 1, 5), (4, 5, 2))
stress_pairs = ((0, 0), (1, 1), (2, 2), (0, 1), (0, 2), (1, 2))
SIZE = 6 * 64 * 72 * 256


def tables():
    fsel = np.zeros((256, 128), np.float32)
    for z in range(64):
        fsel[2 * z, z] = 1
        fsel[128 + 2 * z, 64 + z] = 1
    fedge = np.zeros((2, 384, 128), np.float32)
    fexp = np.zeros((256, NB * 128), np.float32)
    for f in range(3):
        for zi in range(8):
            fedge[0, f * 128 + 2 * (56 + zi), 64 + f * 8 + zi] = 1
            fedge[1, f * 128 + 2 * zi, 88 + f * 8 + zi] = 1
        for block in range(NB):
            for kz in range(10):
                z = block * 8 - 9 + kz
                if -8 <= z < 72:
                    at = f * 64 + z if 0 <= z < 64 else (200 + f * 8 + z if z < 0 else 152 + f * 8 + z)
                    fexp[at, block * 128 + kz * 4 + f] = 1
    texp = np.zeros((768, 1024), np.float32)
    comp = np.zeros((1024, 384), np.float32)
    cedge = np.zeros((2, 128, 128), np.float32)
    cexp = np.zeros((512, NB * 128), np.float32)
    for c in range(6):
        for zi in range(8):
            cedge[0, zi * 16 + c, c * 8 + zi] = 1
            cedge[1, zi * 16 + c, 48 + c * 8 + zi] = 1
            for zb in range(8):
                z = zb * 8 + zi
                texp[c * 128 + 2 * z, zb * 128 + zi * 16 + c] = 1
                comp[zb * 128 + zi * 16 + c, c * 64 + z] = 1
        for block in range(NB):
            for kz in range(10):
                z = block * 8 - 9 + kz
                if -8 <= z < 72:
                    at = c * 64 + z if 0 <= z < 64 else (392 + c * 8 + z if z < 0 else 368 + c * 8 + z)
                    cexp[at, block * 128 + kz * 6 + c] = 1
    vz = np.zeros((2, 1536, 128), np.float32)
    vze = np.zeros((128, 1536), np.float32)
    for p in range(12):
        for k in range(4):
            vz[0, p * 128 + 124 + k, p * 4 + k] = 1
            vz[1, p * 128 + k, 64 + p * 4 + k] = 1
            vze[p * 4 + k, p * 128 + 124 + k] = 1
            vze[64 + p * 4 + k, p * 128 + k] = 1
    pb = np.zeros((144, 160), np.float32)
    for y in range(144):
        at = y // 2
        pb[y, at] = 1
        for shift, value in ((-1, (-7, 1)), (0, (8, -8)), (1, (-1, 7))):
            if 0 <= at + shift < 72:
                pb[y, 80 + at + shift] = value[y % 2]

    def lane(c, z):
        if z < 0:
            return 384 + c * 8 + z + 8
        if z >= 64:
            return 432 + c * 8 + z - 64
        return c * 64 + z

    q1 = np.zeros((1024, 768), np.float32)
    q2 = np.zeros((512, 768), np.float32)
    for i in range(3):
        cx, cy, cz = pair_table[i]
        for z in range(-2, 130):
            out = i * 256 + (z if 0 <= z < 128 else (128 + z - 128 if z >= 128 else 256 + z))
            at = z // 2
            q1[lane(cx, at), out] = 1
            q2[lane(cy, at), out] = 1
            for shift, value in ((-1, (-7, 1)), (0, (8, -8)), (1, (-1, 7))):
                q1[512 + lane(cz, at + shift), out] = value[z % 2]
    spread = np.zeros((16, 128), np.float32)
    for zi in range(8):
        for c in range(16):
            spread[c, zi * 16 + c] = 1
    return [jnp.asarray(t, BF) for t in (fsel, fedge, fexp, texp, comp, cedge, cexp, vz, vze, pb, q1, q2, spread)]


def mm(a, b):
    return jnp.dot(a, b, preferred_element_type=F32)


def lanes(shape):
    return lax.broadcasted_iota(jnp.int32, shape, len(shape) - 1)


def edge_group(dx, z):
    return (7, 1, 3)[dx] if z < 0 else (0, 2, 4)[dx]


def row_of(dx, z):
    return dx * 128 + z * 16 if 0 <= z < 8 else 384 + edge_group(dx, z) * 16


def write_plane(dst, p, value):
    lane = lanes((ROWS, 128))
    dst[p, :, 0:128] = value.astype(BF)
    up = jnp.concatenate([value[RY:], value[:RY]], axis=0)
    down = jnp.concatenate([value[ROWS - RY :], value[: ROWS - RY]], axis=0)
    edge = jnp.where(lane < 16, up, jnp.where(lane >= 112, down, 0.0))
    dst[p, :, 128:256] = edge.astype(BF)
    dst[p, :, 256:384] = pltpu.roll(edge, 32, 1).astype(BF)
    dst[p, :, 384:512] = pltpu.roll(edge, 64, 1).astype(BF)


def window(src, p, rows):
    edges = src[p, rows, 128:256] + src[p + 1, rows, 256:384] + src[p + 2, rows, 384:512]
    return jnp.concatenate([src[p, rows, 0:128], src[p + 1, rows, 0:128], src[p + 2, rows, 0:128], edges], axis=1)


def window_fields(src, p, rows):
    return src[p, rows, 0:128] + src[p + 1, rows, 128:256] + src[p + 2, rows, 256:384]


def window_cot(src, p, rows):
    low, mid, high = (lax.rem(p + 8 + k, 12) for k in range(3))
    return jnp.concatenate([src[low, rows, 0:128] + src[mid, rows, 128:256], src[high, rows, 0:128]], axis=1)


def conv_plane(lhs, kernel):
    r = mm(lhs, kernel)
    return pltpu.roll(r[:, 0:128], 1, 0) + r[:, 128:256] + pltpu.roll(r[:, 256:384], r.shape[0] - 1, 0)


ALL = slice(0, ROWS)
MID = slice(RY, RY + OWN)


def banded(w_in, w_a, w_b, w_out, spread, wt, w1, w4, wf, tiles, flat, turned):
    group = lanes((16, 128)) // 16

    def load(w):
        flat[...] = jnp.zeros((256, 128), F32)
        for n in range(w.shape[0]):
            flat[n * 16 : n * 16 + 16, 0:27] = w[n].astype(F32)

    def turn(first, count, backwards):
        for n in range(count):
            rows = flat[n * 16 : n * 16 + 16] if first else flat[pl.ds(n, 16, stride=16), :]
            turned[n * 32 : n * 32 + 32] = lax.dot_general(
                rows[:, 0:32].astype(BF), spread, (((0,), (0,)), ((), ())), preferred_element_type=F32
            )
        for tap in range(27):
            tiles[tap] = turned[pl.ds(26 - tap if backwards else tap, 16, stride=32), :]

    def fill(out):
        for dx in range(3):
            for dy in range(3):
                at = slice(dy * 128, dy * 128 + 128)
                for z in range(-1, 9):
                    value = jnp.zeros((16, 128), F32)
                    for dz in range(3):
                        value = jnp.where(group == z - (dz - 1), tiles[9 * dx + 3 * dy + dz], value)
                    row = row_of(dx, z)
                    wt[out, row : row + 16, at] = value.astype(BF)
        wt[out, 464:496] = jnp.zeros((32, 384), BF)

    def small(count, starts):
        wf[...] = jnp.zeros((256, 384), F32)
        part = lanes((count, 128)) // 16
        for dx in range(3):
            for dy in range(3):
                for kz in range(10):
                    value = jnp.zeros((count, 128), F32)
                    for dz in range(3):
                        value = jnp.where(part == kz - dz, tiles[9 * dx + 3 * dy + dz, 0:count], value)
                    row = starts[dx] + kz * count
                    wf[row : row + count, dy * 128 : dy * 128 + 128] = value

    load(w_in)
    turn(True, 4, False)
    small(4, (0, 40, 80))
    w1[...] = wf[0:128].astype(BF)
    load(w_a)
    turn(False, 16, False)
    fill(0)
    turn(True, 16, True)
    fill(4)
    load(w_b)
    turn(False, 16, False)
    fill(1)
    turn(True, 16, True)
    fill(3)
    load(w_out)
    turn(False, 16, False)
    fill(2)
    turn(True, 6, True)
    small(6, (0, 60, 128))
    w4[...] = wf[...].astype(BF)


def shifted_cots(cots):
    both = [
        jnp.concatenate([pltpu.roll(c, OWN - 1, 0), c, pltpu.roll(c, 1, 0)], axis=1).astype(BF) for c in cots
    ]
    return jnp.concatenate(both, axis=0)


def keep_tap(gsrc, layer, tap, h):
    group = lanes((16, 128)) // 16
    old = gsrc[layer * 4 + tap // 8] if tap % 8 else jnp.zeros((16, 128), F32)
    gsrc[layer * 4 + tap // 8] = jnp.where(group == tap % 8, h, old)


def weight_gradient(src, first, cots, gsrc, layer, gtmp):
    rhs = jnp.concatenate([window(src, first + x, MID) for x in range(2)], axis=0)
    gtmp[...] = lax.dot_general(shifted_cots(cots), rhs, (((0,), (0,)), ((), ())), preferred_element_type=F32)
    group = lanes((16, 128)) // 16
    for dx in range(3):
        for dy in range(3):
            for dz in range(3):
                h = jnp.zeros((16, 128), F32)
                extra = None
                for zi in range(8):
                    z = zi + dz - 1
                    row = slice(dy * 128 + zi * 16, dy * 128 + zi * 16 + 16)
                    if 0 <= z < 8:
                        h = jnp.where(group == z, gtmp[row, dx * 128 : dx * 128 + 128], h)
                    else:
                        extra = jnp.where(group == edge_group(dx, z), gtmp[row, 384:512], 0.0)
                if extra is not None:
                    h = h + extra
                for step in (64, 32, 16):
                    h = h + pltpu.roll(h, step, 1)
                keep_tap(gsrc, layer, 9 * dx + 3 * dy + dz, h)


def first_gradient(src, first, cots, gsrc, gtmp):
    rhs = jnp.concatenate([window_fields(src, first + x, MID) for x in range(2)], axis=0)
    gtmp[:, 0:128] = lax.dot_general(shifted_cots(cots), rhs, (((0,), (0,)), ((), ())), preferred_element_type=F32)
    part = lanes((16, 128)) // 4
    for dx in range(3):
        for dy in range(3):
            for dz in range(3):
                h = jnp.zeros((16, 128), F32)
                for zi in range(8):
                    row = slice(dy * 128 + zi * 16, dy * 128 + zi * 16 + 16)
                    h = jnp.where(part == dx * 10 + zi + dz, gtmp[row, 0:128], h)
                for step in (112, 120, 124):
                    h = h + pltpu.roll(h, step, 1)
                tap = 9 * dx + 3 * dy + dz
                turn = ((tap % 8) * 16 - (dx * 40 + dz * 4)) % 128
                keep_tap(gsrc, 0, tap, pltpu.roll(h, turn, 1) if turn else h)


def stencil(ref, p, t, r, count, low):
    def at(i, dp, dy):
        return ref[i, p + dp, t, pl.ds(8 + r + dy, count), :]

    vel = [at(i, 0, 0) for i in range(3)]
    outs = []
    for i in range(3):
        f = vel[i]
        other = ref[i, p, 1 - t, pl.ds(8 + r, count), :]
        zp1 = pltpu.roll(jnp.where(low[0], other, f), 127, 1)
        zp2 = pltpu.roll(jnp.where(low[1], other, f), 126, 1)
        zm1 = pltpu.roll(jnp.where(low[2], other, f), 1, 1)
        zm2 = pltpu.roll(jnp.where(low[3], other, f), 2, 1)
        xp1, xp2, xm1, xm2 = at(i, 1, 0), at(i, 2, 0), at(i, -1, 0), at(i, -2, 0)
        yp1, yp2, ym1, ym2 = at(i, 0, 1), at(i, 0, 2), at(i, 0, -1), at(i, 0, -2)
        adv = vel[0] * (8.0 * (xp1 - xm1) - (xp2 - xm2))
        adv = adv + vel[1] * (8.0 * (yp1 - ym1) - (yp2 - ym2))
        adv = adv + vel[2] * (8.0 * (zp1 - zm1) - (zp2 - zm2))
        near = (xp1 + xm1) + (yp1 + ym1) + (zp1 + zm1)
        far = (xp2 + xm2) + (yp2 + ym2) + (zp2 + zm2)
        lap = 8.0 * near - 45.0 * f - 0.5 * far
        outs.append((lap - adv) * (0.1 / 12.0))
    return vel, outs


def body(
    v, w_in, w_a, w_b, w_out, spread, *refs
):
    far = refs[:12]
    vnext, sw, gout = refs[12:15]
    near = refs[15:27]
    fsel, fedge, fexp, texp, comp, cedge, cexp, vz, vze, pb, q1, q2 = near
    (
        fpx, fe, fer, vb, vbx, vzs, vzr, vzf, tx, wt, w1, w4, wf, tiles, flat, turned, xe0, xe1, xe2, xe3, c4, c1, mask,
        cpx, spx, ce, cer, se, ser, gxt, r2s, force, vext, fs, gtmp, gsrc, r1, r2g, csem, ssem, rsem,
    ) = refs[27:]
    held = [pltpu.make_async_copy(far[n], near[n], csem.at[n]) for n in range(12)]
    for copy in held:
        copy.start()
    g = lax.axis_index("grp")
    s = lax.axis_index("slab")
    used = [0]
    sent = []

    def slab_at(k):
        return {"slab": lax.rem(s + (k + SLAB), SLAB)}

    def grp_at(k):
        return {"grp": lax.rem(g + (k + GRP), GRP)}

    def send(src, dst, device):
        k = used[0]
        used[0] += 1
        copy = pltpu.make_async_remote_copy(
            src_ref=src, dst_ref=dst, send_sem=ssem.at[k], recv_sem=rsem.at[k], device_id=device, device_id_type=MESH
        )
        copy.start()
        sent.append(copy)
        return copy

    quad = lax.rem(s, 4)
    a = g * 4 + quad
    b = s // 4

    def peer_a(k):
        other = lax.rem(a + k, 16)
        return other, {"grp": other // 4, "slab": b * 4 + lax.rem(other, 4)}

    def peer_b(k):
        return {"slab": lax.rem(b + k, 8) * 4 + quad}

    barrier = pltpu.get_barrier_semaphore()
    friends = [slab_at(k) for k in (-3, -2, -1, 1, 2, 3)]
    friends += [peer_a(k)[1] for k in range(1, 16)] + [peer_b(k) for k in range(1, 8)]
    for friend in friends:
        pl.semaphore_signal(barrier, inc=1, device_id=friend, device_id_type=MESH)

    held[0].wait()
    held[1].wait()
    parts = []
    blank = jnp.zeros((8, 128), F32)

    def mean(four):
        total = (four[0] + four[1]) + (four[2] + four[3])
        return (total + pltpu.roll(total, 127, 1)) * 0.125

    for X in range(2):
        fine = [[v[c, 2 * X + px, pl.ds(py, 72, stride=2), :] for px in range(2) for py in range(2)] for c in range(3)]
        means = [mean(fine[c]) for c in range(3)]
        parts.append((fine, means))
        fields = [jnp.concatenate([m, blank], axis=0).astype(BF) for m in means]
        fpx[5 + X, :, 0:128] = mm(jnp.concatenate(fields[:2], axis=1), fsel[...]).astype(BF)
        fpx[5 + X, :, 128:256] = mm(fields[2], fsel[0:128]).astype(BF)
        joined = jnp.concatenate(fields, axis=1)
        for side in range(2):
            fe[side, X] = mm(joined, fedge[side]).astype(BF)
    pl.semaphore_wait(barrier, len(friends))
    zc = [send(fe.at[side], fer.at[side], grp_at(k)) for side, k in ((0, 1), (1, -1))]

    fc = []
    fc.append(send(fpx.at[pl.ds(5, 2), :, pl.ds(0, 128)], fpx.at[pl.ds(3, 2), :, pl.ds(0, 128)], slab_at(1)))
    fc.append(send(fpx.at[pl.ds(5, 2), :, pl.ds(0, 128)], fpx.at[pl.ds(7, 2), :, pl.ds(0, 128)], slab_at(-1)))
    fc.append(send(fpx.at[pl.ds(6, 1), :, pl.ds(0, 128)], fpx.at[pl.ds(0, 1), :, pl.ds(0, 128)], slab_at(3)))
    fc.append(send(fpx.at[pl.ds(5, 1), :, pl.ds(0, 128)], fpx.at[pl.ds(11, 1), :, pl.ds(0, 128)], slab_at(-3)))
    fc.append(send(fpx.at[pl.ds(5, 2), :, pl.ds(0, 128)], fpx.at[pl.ds(1, 2), :, pl.ds(0, 128)], slab_at(2)))
    fc.append(send(fpx.at[pl.ds(5, 2), :, pl.ds(0, 128)], fpx.at[pl.ds(9, 2), :, pl.ds(0, 128)], slab_at(-2)))

    vb[...] = v[...].astype(BF)
    held[7].wait()
    joined = jnp.concatenate([vb[c, x] for c in range(3) for x in range(4)], axis=1)
    for side in range(2):
        vzs[side] = mm(joined, vz[side]).astype(BF)
    uc = [send(vzs.at[side], vzr.at[side], grp_at(k)) for side, k in ((0, 1), (1, -1))]

    for copy in zc:
        copy.wait_recv()
    for X in range(2):
        fpx[5 + X, :, 128:256] = fpx[5 + X, :, 128:256] + fer[0, X] + fer[1, X]
    fc.append(send(fpx.at[pl.ds(5, 2), :, pl.ds(128, 128)], fpx.at[pl.ds(3, 2), :, pl.ds(128, 128)], slab_at(1)))
    fc.append(send(fpx.at[pl.ds(5, 2), :, pl.ds(128, 128)], fpx.at[pl.ds(7, 2), :, pl.ds(128, 128)], slab_at(-1)))
    fc.append(send(fpx.at[pl.ds(6, 1), :, pl.ds(128, 128)], fpx.at[pl.ds(0, 1), :, pl.ds(128, 128)], slab_at(3)))
    fc.append(send(fpx.at[pl.ds(5, 1), :, pl.ds(128, 128)], fpx.at[pl.ds(11, 1), :, pl.ds(128, 128)], slab_at(-3)))
    fc.append(send(fpx.at[pl.ds(5, 2), :, pl.ds(128, 128)], fpx.at[pl.ds(1, 2), :, pl.ds(128, 128)], slab_at(2)))
    fc.append(send(fpx.at[pl.ds(5, 2), :, pl.ds(128, 128)], fpx.at[pl.ds(9, 2), :, pl.ds(128, 128)], slab_at(-2)))

    banded(w_in, w_a, w_b, w_out, spread[...], wt, w1, w4, wf, tiles, flat, turned)
    for zb in range(NB):
        mask[zb * RY : zb * RY + 72] = jnp.ones((72, 128), F32)
        mask[zb * RY + 72 : zb * RY + RY] = jnp.zeros((8, 128), F32)
    held[3].wait()
    for X in range(2):
        fine, means = parts[X]
        targets = []
        for i, j in stress_pairs:
            t = mean([fine[i][n] * fine[j][n] for n in range(4)]) - means[i] * means[j]
            targets.append(jnp.concatenate([t, blank], axis=0).astype(BF))
        t = mm(jnp.concatenate(targets, axis=1), texp[...])
        for zb in range(8):
            tx[X, zb * RY : zb * RY + RY] = t[:, zb * 128 : zb * 128 + 128]
    pads = jnp.zeros((8, 128), F32)
    for c in range(3):

        @pl.loop(0, 12)
        def _(p, c=c):
            for t in range(2):
                vext[c, p, t, 0:8] = pads
                vext[c, p, t, 152:160] = pads

        @pl.loop(0, 8)
        def _(p, c=c):
            for t in range(2):
                fs[c, p, t, 0:8] = pads
                fs[c, p, t, 152:160] = pads

        for x in range(4):
            vext[c, 4 + x, 0, 8:152] = v[c, x]

    for copy in uc:
        copy.wait_recv()
    vzf[1] = vzr[0] + vzr[1]
    for copy in fc:
        copy.wait_recv()
    vc = []
    for place, k in ((0, 1), (1, -1)):
        vc.append(send(vb, vbx.at[place], slab_at(k)))
        vc.append(send(vzf.at[1], vzf.at[2 * place], slab_at(k)))

    def expand(src, table, dst, count, shifts, start):
        width = src.shape[2]

        @pl.loop(0, count // 4)
        def _(q):
            r = mm(src[pl.ds(q * 4, 4)].reshape(4 * RY, width), table[...])
            for n in range(4):
                for zb in range(NB):
                    block = r[n * RY : n * RY + RY, zb * 128 : zb * 128 + 128]
                    for m, shift in enumerate(shifts):
                        moved = pltpu.roll(block, shift, 1) if shift else block
                        dst[lax.rem(q * 4 + start, 12) + n, zb * RY : zb * RY + RY, m * 128 : m * 128 + 128] = moved.astype(BF)

    held[2].wait()
    expand(fpx, fexp, xe0, 12, (0, 40, 80), 0)

    @pl.loop(0, 10)
    def _(p):
        write_plane(xe1, p, jnp.tanh(conv_plane(window_fields(xe0, p, ALL), w1[...])) * mask[...])

    for k, (src, dst, count) in enumerate(((xe1, xe2, 8), (xe2, xe3, 6))):

        @pl.loop(0, count)
        def _(p, src=src, dst=dst, k=k):
            write_plane(dst, p, jnp.tanh(conv_plane(window(src, p, ALL), wt[k])) * mask[...])

    held[4].wait()
    held[5].wait()
    for X in range(2):
        pred = conv_plane(window(xe3, X + 1, MID), wt[2]) * mask[MID]
        stress = pred.astype(BF)
        cot = (2.0 / SIZE * (pred - tx[X])).astype(BF)
        c4[X] = cot.astype(F32)
        for value, pack, edges, at in ((cot, cpx, ce, 3), (stress, spx, se, 2)):
            joined = jnp.concatenate([value[zb * RY : zb * RY + RY] for zb in range(8)], axis=1)
            pack[at + X, :, 0:384] = mm(joined, comp[...]).astype(BF)
            edges[0, X] = mm(value[7 * RY : 8 * RY], cedge[0]).astype(BF)
            edges[1, X] = mm(value[0:RY], cedge[1]).astype(BF)

    zc = []
    for side, k in ((0, 1), (1, -1)):
        zc.append(send(ce.at[side], cer.at[side], grp_at(k)))
        zc.append(send(se.at[side], ser.at[side], grp_at(k)))
    cc = []
    cc.append(send(cpx.at[pl.ds(3, 2), :, pl.ds(0, 384)], cpx.at[pl.ds(1, 2), :, pl.ds(0, 384)], slab_at(1)))
    cc.append(send(cpx.at[pl.ds(3, 2), :, pl.ds(0, 384)], cpx.at[pl.ds(5, 2), :, pl.ds(0, 384)], slab_at(-1)))
    cc.append(send(cpx.at[pl.ds(4, 1), :, pl.ds(0, 384)], cpx.at[pl.ds(0, 1), :, pl.ds(0, 384)], slab_at(2)))
    cc.append(send(cpx.at[pl.ds(3, 1), :, pl.ds(0, 384)], cpx.at[pl.ds(7, 1), :, pl.ds(0, 384)], slab_at(-2)))
    weight_gradient(xe3, 1, [c4[0], c4[1]], gsrc, 3, gtmp)

    for copy in zc:
        copy.wait_recv()
    for X in range(2):
        cpx[3 + X, :, 384:512] = cer[0, X] + cer[1, X]
        spx[2 + X, :, 384:512] = ser[0, X] + ser[1, X]
    cc.append(send(cpx.at[pl.ds(3, 2), :, pl.ds(384, 128)], cpx.at[pl.ds(1, 2), :, pl.ds(384, 128)], slab_at(1)))
    cc.append(send(cpx.at[pl.ds(3, 2), :, pl.ds(384, 128)], cpx.at[pl.ds(5, 2), :, pl.ds(384, 128)], slab_at(-1)))
    cc.append(send(cpx.at[pl.ds(4, 1), :, pl.ds(384, 128)], cpx.at[pl.ds(0, 1), :, pl.ds(384, 128)], slab_at(2)))
    cc.append(send(cpx.at[pl.ds(3, 1), :, pl.ds(384, 128)], cpx.at[pl.ds(7, 1), :, pl.ds(384, 128)], slab_at(-2)))

    for copy in vc:
        copy.wait_recv()
    for c in range(3):
        for x in range(4):
            vext[c, x, 0, 8:152] = vbx[0, c, x].astype(F32)
            vext[c, 8 + x, 0, 8:152] = vbx[1, c, x].astype(F32)
    held[8].wait()
    for n in range(3):
        r = mm(vzf[n], vze[...])
        for c in range(3):
            for x in range(4):
                p = c * 4 + x
                vext[c, 4 * n + x, 1, 8:152] = r[:, p * 128 : p * 128 + 128]

    count = 48
    lane = lanes((count, 128))
    low = (lane < 1, lane < 2, lane >= 127, lane >= 126)

    def first_step(start, stop):
        @pl.loop(start, stop)
        def _(p):
            for t in range(2):
                for r in range(0, 144, count):
                    vel, outs = stencil(vext, p + 2, t, r, count, low)
                    for i in range(3):
                        fs[i, p, t, 8 + r : 8 + r + count] = vel[i] + outs[i]

    first_step(0, 3)
    for copy in cc:
        copy.wait_recv()
    sc = []
    sc.append(send(spx.at[pl.ds(2, 2)], spx.at[pl.ds(0, 2)], slab_at(1)))
    sc.append(send(spx.at[pl.ds(2, 2)], spx.at[pl.ds(4, 2)], slab_at(-1)))
    wc = []
    for k in range(1, GRP):
        other = lax.rem(g + k, GRP)
        rows = pl.ds(pl.multiple_of(other * 16, 16), 32)
        wc.append(send(spx.at[pl.ds(2, 2), rows, pl.ds(0, 384)], sw.at[g], grp_at(k)))
    rows = pl.ds(pl.multiple_of(g * 16, 16), 32)
    sw[g] = spx[2:4, rows, 0:384]

    held[6].wait()
    expand(cpx, cexp, xe0, 8, (0, 60), 8)

    def damp(act, p, rows=ALL):
        below = act[p, rows, 0:128].astype(F32)
        return (1.0 - below * below) * mask[rows]

    @pl.loop(0, 6)
    def _(p):
        write_plane(xe3, p, conv_plane(window_cot(xe0, p, ALL), w4[...]) * damp(xe3, p))

    def own(ref, at):
        return [ref[at + X, MID, 0:128].astype(F32) for X in range(2)]

    weight_gradient(xe2, 2, own(xe3, 2), gsrc, 2, gtmp)

    @pl.loop(0, 4)
    def _(p):
        write_plane(xe2, p + 2, conv_plane(window(xe3, p, ALL), wt[3]) * damp(xe2, p + 2))

    weight_gradient(xe1, 3, own(xe2, 3), gsrc, 1, gtmp)
    for X in range(2):
        c1[X] = (conv_plane(window(xe2, X + 2, MID), wt[4]) * damp(xe1, X + 4, MID)).astype(BF).astype(F32)
    first_gradient(xe0, 4, [c1[0], c1[1]], gsrc, gtmp)

    first = [send(gsrc.at[peer_a(k)[0]], r1.at[k - 1], peer_a(k)[1]) for k in range(1, 16)]

    first_step(3, 8)
    for copy in first:
        copy.wait_recv()
    total = gsrc[a]
    for k in range(15):
        total = total + r1[k]
    r2g[b] = total
    second = [send(r2g.at[b], r2g.at[b], peer_b(k)) for k in range(1, 8)]

    for copy in sc:
        copy.wait_recv()
    for n in (9, 10, 11):
        held[n].wait()
    for n in range(8):
        at = 1 + n // 2
        lower, mid, upper = (spx[at + d].astype(F32) for d in (-1, 0, 1))
        if n % 2 == 0:
            slope = 8.0 * mid - upper - 7.0 * lower
        else:
            slope = 7.0 * upper - 8.0 * mid + lower
        gxt[n * RY : n * RY + RY, 0:512] = slope.astype(BF)
        gxt[n * RY : n * RY + RY, 512:1024] = spx[at]
        if n % 2 == 0:
            r2s[n // 2] = mm(spx[at], q2[...]).astype(BF)
    r = mm(gxt[...], q1[...]).astype(BF)
    for n in range(8):
        both = jnp.concatenate([r[n * RY : n * RY + RY], r2s[n // 2]], axis=0)
        force[n] = mm(pb[...], both) * (-4.0 / 12.0)

    for copy in second:
        copy.wait_recv()
    total = r2g[0]
    for k in range(1, 8):
        total = total + r2g[k]
    gout[a] = total
    third = [send(gout.at[a], gout.at[a], peer_a(k)[1]) for k in range(1, 16)]

    @pl.loop(0, 8)
    def _(p):
        for t in range(2):
            for i in range(3):
                at = i * 256 + t * 128
                fs[i, p, t, 8:152] = fs[i, p, t, 8:152] + 0.1 * force[p, :, at : at + 128]

    @pl.loop(0, 4)
    def _(x):
        for r in range(0, 144, count):
            vel, outs = stencil(fs, x + 2, 0, r, count, low)
            for i in range(3):
                again = outs[i] + 0.1 * force[x + 2, r : r + count, i * 256 : i * 256 + 128]
                vnext[i, x, r : r + count] = 0.5 * (v[i, x, r : r + count] + vel[i] + again)

    for copy in third:
        copy.wait_recv()
    for copy in wc:
        copy.wait_recv()
    for copy in sent:
        copy.wait_send()


def finish(vnext, sw, gout, vout, stress, g0, g1, g2, g3, rows, taps):
    vout[...] = vnext[...]
    start = 2 * lax.axis_index("grp")
    low = lanes((18, 128)) < 64
    for tile in range(3):
        rows[tile] = sw[:, :, :, tile * 128 : tile * 128 + 128].astype(F32)
    for c in range(6):
        for half in range(2):
            planes = []
            for x in range(2):
                left = rows[c // 2, 2 * half, x, pl.ds(start, 18), :]
                right = rows[c // 2, 2 * half + 1, x, pl.ds(start, 18), :]
                if c % 2:
                    left = pltpu.roll(left, 64, 1)
                else:
                    right = pltpu.roll(right, 64, 1)
                planes.append(jnp.where(low, left, right))
            stress[c, :, :, half * 128 : half * 128 + 128] = jnp.stack(planes, axis=1).astype(BF)
    for layer, out in enumerate((g0, g1, g2, g3)):
        for tap in range(27):
            tile = gout[layer * 4 + tap // 8]
            shift = (128 - tap % 8 * 16) % 128
            taps[tap * 16 : tap * 16 + 16] = pltpu.roll(tile, shift, 1) if shift else tile
        for n in range(16 if layer == 0 else out.shape[0]):
            turned = jnp.transpose(taps[pl.ds(n, 32, stride=16), :])
            if layer == 0:
                for q in range(3):
                    out[q, n : n + 1] = turned[q : q + 1, 0:27]
            else:
                out[n] = turned[0:16, 0:27]


def local(velocity, w_in, w_mid_a, w_mid_b, w_out):
    vm = pltpu.VMEM
    scratch = [
        vm((12, RY, 256), BF), vm((2, 2, RY, 128), BF), vm((2, 2, RY, 128), BF),
        vm((3, 4, 144, 128), BF), vm((2, 3, 4, 144, 128), BF),
        vm((2, 144, 128), BF), vm((2, 144, 128), BF), vm((3, 144, 128), BF),
        vm((2, OWN, 128), F32), vm((5, 512, 384), BF),
        vm((128, 384), BF), vm((256, 384), BF), vm((256, 384), F32), vm((27, 16, 128), F32),
        vm((256, 128), F32), vm((512, 128), F32),
        vm((12, ROWS, 384), BF), vm((10, ROWS, 512), BF), vm((8, ROWS, 512), BF), vm((6, ROWS, 512), BF),
        vm((2, OWN, 128), F32),
        vm((2, OWN, 128), F32),
        vm((ROWS, 128), F32),
        vm((8, RY, 512), BF), vm((6, RY, 512), BF),
        vm((2, 2, RY, 128), BF), vm((2, 2, RY, 128), BF), vm((2, 2, RY, 128), BF), vm((2, 2, RY, 128), BF),
        vm((8 * RY, 1024), BF), vm((4, RY, 768), BF), vm((8, 144, 768), F32),
        vm((3, 12, 2, 160, 128), F32), vm((3, 8, 2, 160, 128), F32),
        vm((384, 512), F32), vm((16, 16, 128), F32), vm((15, 16, 128), F32), vm((8, 16, 128), F32),
        pltpu.SemaphoreType.DMA((12,)), pltpu.SemaphoreType.DMA((80,)), pltpu.SemaphoreType.DMA((80,)),
    ]
    *consts, spread = tables()
    scratch = [vm(t.shape, BF) for t in consts] + scratch
    inside = pl.BlockSpec(memory_space=pltpu.VMEM)
    vnext, sw, gout = pl.pallas_call(
        body,
        out_shape=[
            jax.ShapeDtypeStruct((3, 4, 144, 128), F32),
            jax.ShapeDtypeStruct((4, 2, 32, 384), BF),
            jax.ShapeDtypeStruct((16, 16, 128), F32),
        ],
        in_specs=[inside] * 6 + [pl.BlockSpec(memory_space=pl.ANY)] * len(consts),
        out_specs=[inside] * 3,
        scratch_shapes=scratch,
        compiler_params=pltpu.CompilerParams(
            collective_id=0, has_side_effects=True, vmem_limit_bytes=62 * 1024 * 1024
        ),
    )(
        velocity,
        jnp.transpose(w_in, (2, 1, 0)),
        *(jnp.transpose(w, (1, 2, 0)) for w in (w_mid_a, w_mid_b, w_out)),
        spread,
        *consts,
    )
    shapes = [((3, 4, 144, 128), F32), ((6, 18, 2, 256), BF)]
    shapes += [((3, 16, 27), F32), ((16, 16, 27), F32), ((16, 16, 27), F32), ((6, 16, 27), F32)]
    vnext, stress, g0, *rest = pl.pallas_call(
        finish,
        out_shape=[jax.ShapeDtypeStruct(*shape) for shape in shapes],
        in_specs=[inside] * 3,
        out_specs=[inside] * 6,
        scratch_shapes=[vm((3, 4, 2, 32, 128), F32), vm((512, 128), F32)],
        compiler_params=pltpu.CompilerParams(vmem_limit_bytes=60 * 1024 * 1024),
    )(vnext, sw, gout)
    stress = jnp.transpose(stress, (0, 2, 1, 3))
    return (vnext, stress, jnp.transpose(g0, (2, 1, 0)), *(jnp.transpose(g, (2, 0, 1)) for g in rest))


def solution(mesh):
    in_specs = (P(None, "slab", None, "grp"), P(), P(), P(), P())
    out_specs = (P(None, "slab", None, "grp"), P(None, "slab", "grp", None), P(), P(), P(), P())
    return jax.shard_map(local, mesh=mesh, in_specs=in_specs, out_specs=out_specs, check_vma=False)
```

```python
import jax
import jax.numpy as jnp
import numpy as np
from jax import lax
from jax.experimental import pallas as pl
from jax.experimental.pallas import tpu as pltpu
from jax.sharding import PartitionSpec as P

MESH = pl.DeviceIdType.MESH
F32 = jnp.float32
BF = jnp.bfloat16
GRP, SLAB = 4, 32
RY = 80
NB = 10
ROWS = NB * RY
OWN = 8 * RY
pair_table = ((0, 3, 4), (3, 1, 5), (4, 5, 2))
stress_pairs = ((0, 0), (1, 1), (2, 2), (0, 1), (0, 2), (1, 2))
SIZE = 6 * 64 * 72 * 256


def tables():
    fsel = np.zeros((256, 128), np.float32)
    for z in range(64):
        fsel[2 * z, z] = 1
        fsel[128 + 2 * z, 64 + z] = 1
    fedge = np.zeros((2, 384, 128), np.float32)
    fexp = np.zeros((256, NB * 128), np.float32)
    for f in range(3):
        for zi in range(8):
            fedge[0, f * 128 + 2 * (56 + zi), 64 + f * 8 + zi] = 1
            fedge[1, f * 128 + 2 * zi, 88 + f * 8 + zi] = 1
        for block in range(NB):
            for kz in range(10):
                z = block * 8 - 9 + kz
                if -8 <= z < 72:
                    at = f * 64 + z if 0 <= z < 64 else (200 + f * 8 + z if z < 0 else 152 + f * 8 + z)
                    fexp[at, block * 128 + kz * 4 + f] = 1
    texp = np.zeros((768, 1024), np.float32)
    comp = np.zeros((1024, 384), np.float32)
    cedge = np.zeros((2, 128, 128), np.float32)
    cexp = np.zeros((512, NB * 128), np.float32)
    for c in range(6):
        for zi in range(8):
            cedge[0, zi * 16 + c, c * 8 + zi] = 1
            cedge[1, zi * 16 + c, 48 + c * 8 + zi] = 1
            for zb in range(8):
                z = zb * 8 + zi
                texp[c * 128 + 2 * z, zb * 128 + zi * 16 + c] = 1
                comp[zb * 128 + zi * 16 + c, c * 64 + z] = 1
        for block in range(NB):
            for kz in range(10):
                z = block * 8 - 9 + kz
                if -8 <= z < 72:
                    at = c * 64 + z if 0 <= z < 64 else (392 + c * 8 + z if z < 0 else 368 + c * 8 + z)
                    cexp[at, block * 128 + kz * 6 + c] = 1
    vz = np.zeros((2, 1536, 128), np.float32)
    vze = np.zeros((128, 1536), np.float32)
    for p in range(12):
        for k in range(4):
            vz[0, p * 128 + 124 + k, p * 4 + k] = 1
            vz[1, p * 128 + k, 64 + p * 4 + k] = 1
            vze[p * 4 + k, p * 128 + 124 + k] = 1
            vze[64 + p * 4 + k, p * 128 + k] = 1
    pb = np.zeros((144, 160), np.float32)
    for y in range(144):
        at = y // 2
        pb[y, at] = 1
        for shift, value in ((-1, (-7, 1)), (0, (8, -8)), (1, (-1, 7))):
            if 0 <= at + shift < 72:
                pb[y, 80 + at + shift] = value[y % 2]

    def lane(c, z):
        if z < 0:
            return 384 + c * 8 + z + 8
        if z >= 64:
            return 432 + c * 8 + z - 64
        return c * 64 + z

    q1 = np.zeros((1024, 768), np.float32)
    q2 = np.zeros((512, 768), np.float32)
    for i in range(3):
        cx, cy, cz = pair_table[i]
        for z in range(-2, 130):
            out = i * 256 + (z if 0 <= z < 128 else (128 + z - 128 if z >= 128 else 256 + z))
            at = z // 2
            q1[lane(cx, at), out] = 1
            q2[lane(cy, at), out] = 1
            for shift, value in ((-1, (-7, 1)), (0, (8, -8)), (1, (-1, 7))):
                q1[512 + lane(cz, at + shift), out] = value[z % 2]
    spread = np.zeros((16, 128), np.float32)
    for zi in range(8):
        for c in range(16):
            spread[c, zi * 16 + c] = 1
    return [jnp.asarray(t, BF) for t in (fsel, fedge, fexp, texp, comp, cedge, cexp, vz, vze, pb, q1, q2, spread)]


def mm(a, b):
    return jnp.dot(a, b, preferred_element_type=F32)


def lanes(shape):
    return lax.broadcasted_iota(jnp.int32, shape, len(shape) - 1)


def edge_group(dx, z):
    return (7, 1, 3)[dx] if z < 0 else (0, 2, 4)[dx]


def row_of(dx, z):
    return dx * 128 + z * 16 if 0 <= z < 8 else 384 + edge_group(dx, z) * 16


def write_plane(dst, p, value):
    lane = lanes((ROWS, 128))
    dst[p, :, 0:128] = value.astype(BF)
    up = jnp.concatenate([value[RY:], value[:RY]], axis=0)
    down = jnp.concatenate([value[ROWS - RY :], value[: ROWS - RY]], axis=0)
    edge = jnp.where(lane < 16, up, jnp.where(lane >= 112, down, 0.0))
    dst[p, :, 128:256] = edge.astype(BF)
    dst[p, :, 256:384] = pltpu.roll(edge, 32, 1).astype(BF)
    dst[p, :, 384:512] = pltpu.roll(edge, 64, 1).astype(BF)


def window(src, p, rows):
    edges = src[p, rows, 128:256] + src[p + 1, rows, 256:384] + src[p + 2, rows, 384:512]
    return jnp.concatenate([src[p, rows, 0:128], src[p + 1, rows, 0:128], src[p + 2, rows, 0:128], edges], axis=1)


def window_fields(src, p, rows):
    return src[p, rows, 0:128] + src[p + 1, rows, 128:256] + src[p + 2, rows, 256:384]


def window_cot(src, p, rows):
    low, mid, high = (lax.rem(p + 8 + k, 12) for k in range(3))
    return jnp.concatenate([src[low, rows, 0:128] + src[mid, rows, 128:256], src[high, rows, 0:128]], axis=1)


def conv_plane(lhs, kernel):
    r = mm(lhs, kernel)
    return pltpu.roll(r[:, 0:128], 1, 0) + r[:, 128:256] + pltpu.roll(r[:, 256:384], r.shape[0] - 1, 0)


ALL = slice(0, ROWS)
MID = slice(RY, RY + OWN)


def banded(w_in, w_a, w_b, w_out, spread, wt, w1, w4, wf, tiles, flat, turned):
    group = lanes((16, 128)) // 16

    def load(w):
        flat[...] = jnp.zeros((256, 128), F32)
        for n in range(w.shape[0]):
            flat[n * 16 : n * 16 + 16, 0:27] = w[n].astype(F32)

    def turn(first, count, backwards):
        for n in range(count):
            rows = flat[n * 16 : n * 16 + 16] if first else flat[pl.ds(n, 16, stride=16), :]
            turned[n * 32 : n * 32 + 32] = lax.dot_general(
                rows[:, 0:32].astype(BF), spread, (((0,), (0,)), ((), ())), preferred_element_type=F32
            )
        for tap in range(27):
            tiles[tap] = turned[pl.ds(26 - tap if backwards else tap, 16, stride=32), :]

    def fill(out):
        for dx in range(3):
            for dy in range(3):
                at = slice(dy * 128, dy * 128 + 128)
                for z in range(-1, 9):
                    value = jnp.zeros((16, 128), F32)
                    for dz in range(3):
                        value = jnp.where(group == z - (dz - 1), tiles[9 * dx + 3 * dy + dz], value)
                    row = row_of(dx, z)
                    wt[out, row : row + 16, at] = value.astype(BF)
        wt[out, 464:496] = jnp.zeros((32, 384), BF)

    def small(count, starts):
        wf[...] = jnp.zeros((256, 384), F32)
        part = lanes((count, 128)) // 16
        for dx in range(3):
            for dy in range(3):
                for kz in range(10):
                    value = jnp.zeros((count, 128), F32)
                    for dz in range(3):
                        value = jnp.where(part == kz - dz, tiles[9 * dx + 3 * dy + dz, 0:count], value)
                    row = starts[dx] + kz * count
                    wf[row : row + count, dy * 128 : dy * 128 + 128] = value

    load(w_in)
    turn(True, 4, False)
    small(4, (0, 40, 80))
    w1[...] = wf[0:128].astype(BF)
    load(w_a)
    turn(False, 16, False)
    fill(0)
    turn(True, 16, True)
    fill(4)
    load(w_b)
    turn(False, 16, False)
    fill(1)
    turn(True, 16, True)
    fill(3)
    load(w_out)
    turn(False, 16, False)
    fill(2)
    turn(True, 6, True)
    small(6, (0, 60, 128))
    w4[...] = wf[...].astype(BF)


def shifted_cots(cots):
    both = [
        jnp.concatenate([pltpu.roll(c, OWN - 1, 0), c, pltpu.roll(c, 1, 0)], axis=1).astype(BF) for c in cots
    ]
    return jnp.concatenate(both, axis=0)


def keep_taps(gsrc, layer, one):
    group = lanes((16, 128)) // 16
    tile = None
    for tap in range(27):
        h = one(tap // 9, tap // 3 % 3, tap % 3, tap)
        tile = jnp.where(group == tap % 8, h, tile) if tap % 8 else h
        if tap % 8 == 7 or tap == 26:
            gsrc[layer * 4 + tap // 8] = tile


def weight_gradient(src, first, cots, gsrc, layer, gtmp):
    rhs = jnp.concatenate([window(src, first + x, MID) for x in range(2)], axis=0)
    gtmp[...] = lax.dot_general(shifted_cots(cots), rhs, (((0,), (0,)), ((), ())), preferred_element_type=F32)
    group = lanes((16, 128)) // 16

    def one(dx, dy, dz, tap):
        h = jnp.zeros((16, 128), F32)
        extra = None
        for zi in range(8):
            z = zi + dz - 1
            row = slice(dy * 128 + zi * 16, dy * 128 + zi * 16 + 16)
            if 0 <= z < 8:
                h = jnp.where(group == z, gtmp[row, dx * 128 : dx * 128 + 128], h)
            else:
                extra = jnp.where(group == edge_group(dx, z), gtmp[row, 384:512], 0.0)
        if extra is not None:
            h = h + extra
        for step in (64, 32, 16):
            h = h + pltpu.roll(h, step, 1)
        return h

    keep_taps(gsrc, layer, one)


def first_gradient(src, first, cots, gsrc, gtmp):
    rhs = jnp.concatenate([window_fields(src, first + x, MID) for x in range(2)], axis=0)
    gtmp[:, 0:128] = lax.dot_general(shifted_cots(cots), rhs, (((0,), (0,)), ((), ())), preferred_element_type=F32)
    part = lanes((16, 128)) // 4

    def one(dx, dy, dz, tap):
        h = jnp.zeros((16, 128), F32)
        for zi in range(8):
            row = slice(dy * 128 + zi * 16, dy * 128 + zi * 16 + 16)
            h = jnp.where(part == dx * 10 + zi + dz, gtmp[row, 0:128], h)
        for step in (112, 120, 124):
            h = h + pltpu.roll(h, step, 1)
        turn = ((tap % 8) * 16 - (dx * 40 + dz * 4)) % 128
        return pltpu.roll(h, turn, 1) if turn else h

    keep_taps(gsrc, 0, one)


def stencil(ref, p, t, r, count, low):
    def at(i, dp, dy):
        return ref[i, p + dp, t, pl.ds(8 + r + dy, count), :]

    vel = [at(i, 0, 0) for i in range(3)]
    outs = []
    for i in range(3):
        f = vel[i]
        other = ref[i, p, 1 - t, pl.ds(8 + r, count), :]
        zp1 = pltpu.roll(jnp.where(low[0], other, f), 127, 1)
        zp2 = pltpu.roll(jnp.where(low[1], other, f), 126, 1)
        zm1 = pltpu.roll(jnp.where(low[2], other, f), 1, 1)
        zm2 = pltpu.roll(jnp.where(low[3], other, f), 2, 1)
        xp1, xp2, xm1, xm2 = at(i, 1, 0), at(i, 2, 0), at(i, -1, 0), at(i, -2, 0)
        yp1, yp2, ym1, ym2 = at(i, 0, 1), at(i, 0, 2), at(i, 0, -1), at(i, 0, -2)
        adv = vel[0] * (8.0 * (xp1 - xm1) - (xp2 - xm2))
        adv = adv + vel[1] * (8.0 * (yp1 - ym1) - (yp2 - ym2))
        adv = adv + vel[2] * (8.0 * (zp1 - zm1) - (zp2 - zm2))
        near = (xp1 + xm1) + (yp1 + ym1) + (zp1 + zm1)
        far = (xp2 + xm2) + (yp2 + ym2) + (zp2 + zm2)
        lap = 8.0 * near - 45.0 * f - 0.5 * far
        outs.append((lap - adv) * (0.1 / 12.0))
    return vel, outs


def body(
    v, w_in, w_a, w_b, w_out, spread, *refs
):
    far = refs[:12]
    vnext, sw, gout = refs[12:15]
    near = refs[15:27]
    fsel, fedge, fexp, texp, comp, cedge, cexp, vz, vze, pb, q1, q2 = near
    (
        fpx, fe, fer, vb, vbx, vzs, vzr, vzf, tx, wt, w1, w4, wf, tiles, flat, turned, xe0, xe1, xe2, xe3, c4, c1, mask,
        cpx, spx, ce, cer, se, ser, gxt, r2s, force, vext, fs, gtmp, gsrc, r1, r2g, csem, ssem, rsem,
    ) = refs[27:]
    held = [pltpu.make_async_copy(far[n], near[n], csem.at[n]) for n in range(12)]
    for copy in held:
        copy.start()
    g = lax.axis_index("grp")
    s = lax.axis_index("slab")
    used = [0]
    sent = []

    def slab_at(k):
        return {"slab": lax.rem(s + (k + SLAB), SLAB)}

    def grp_at(k):
        return {"grp": lax.rem(g + (k + GRP), GRP)}

    def send(src, dst, device):
        k = used[0]
        used[0] += 1
        copy = pltpu.make_async_remote_copy(
            src_ref=src, dst_ref=dst, send_sem=ssem.at[k], recv_sem=rsem.at[k], device_id=device, device_id_type=MESH
        )
        copy.start()
        sent.append(copy)
        return copy

    quad = lax.rem(s, 4)
    a = g * 4 + quad
    b = s // 4

    def peer_a(k):
        other = lax.rem(a + k, 16)
        return other, {"grp": other // 4, "slab": b * 4 + lax.rem(other, 4)}

    def peer_b(k):
        return {"slab": lax.rem(b + k, 8) * 4 + quad}

    barrier = pltpu.get_barrier_semaphore()
    friends = [slab_at(k) for k in (-3, -2, -1, 1, 2, 3)]
    friends += [peer_a(k)[1] for k in range(1, 16)] + [peer_b(k) for k in range(1, 8)]
    for friend in friends:
        pl.semaphore_signal(barrier, inc=1, device_id=friend, device_id_type=MESH)

    held[0].wait()
    held[1].wait()
    parts = []
    blank = jnp.zeros((8, 128), F32)

    def mean(four):
        total = (four[0] + four[1]) + (four[2] + four[3])
        return (total + pltpu.roll(total, 127, 1)) * 0.125

    for X in range(2):
        fine = [[v[c, 2 * X + px, pl.ds(py, 72, stride=2), :] for px in range(2) for py in range(2)] for c in range(3)]
        means = [mean(fine[c]) for c in range(3)]
        parts.append((fine, means))
        fields = [jnp.concatenate([m, blank], axis=0).astype(BF) for m in means]
        fpx[5 + X, :, 0:128] = mm(jnp.concatenate(fields[:2], axis=1), fsel[...]).astype(BF)
        fpx[5 + X, :, 128:256] = mm(fields[2], fsel[0:128]).astype(BF)
        joined = jnp.concatenate(fields, axis=1)
        for side in range(2):
            fe[side, X] = mm(joined, fedge[side]).astype(BF)
    pl.semaphore_wait(barrier, len(friends))
    zc = [send(fe.at[side], fer.at[side], grp_at(k)) for side, k in ((0, 1), (1, -1))]

    fc = []
    fc.append(send(fpx.at[pl.ds(5, 2), :, pl.ds(0, 128)], fpx.at[pl.ds(3, 2), :, pl.ds(0, 128)], slab_at(1)))
    fc.append(send(fpx.at[pl.ds(5, 2), :, pl.ds(0, 128)], fpx.at[pl.ds(7, 2), :, pl.ds(0, 128)], slab_at(-1)))
    fc.append(send(fpx.at[pl.ds(6, 1), :, pl.ds(0, 128)], fpx.at[pl.ds(0, 1), :, pl.ds(0, 128)], slab_at(3)))
    fc.append(send(fpx.at[pl.ds(5, 1), :, pl.ds(0, 128)], fpx.at[pl.ds(11, 1), :, pl.ds(0, 128)], slab_at(-3)))
    fc.append(send(fpx.at[pl.ds(5, 2), :, pl.ds(0, 128)], fpx.at[pl.ds(1, 2), :, pl.ds(0, 128)], slab_at(2)))
    fc.append(send(fpx.at[pl.ds(5, 2), :, pl.ds(0, 128)], fpx.at[pl.ds(9, 2), :, pl.ds(0, 128)], slab_at(-2)))

    vb[...] = v[...].astype(BF)
    held[7].wait()
    joined = jnp.concatenate([vb[c, x] for c in range(3) for x in range(4)], axis=1)
    for side in range(2):
        vzs[side] = mm(joined, vz[side]).astype(BF)
    uc = [send(vzs.at[side], vzr.at[side], grp_at(k)) for side, k in ((0, 1), (1, -1))]

    for copy in zc:
        copy.wait_recv()
    for X in range(2):
        fpx[5 + X, :, 128:256] = fpx[5 + X, :, 128:256] + fer[0, X] + fer[1, X]
    fc.append(send(fpx.at[pl.ds(5, 2), :, pl.ds(128, 128)], fpx.at[pl.ds(3, 2), :, pl.ds(128, 128)], slab_at(1)))
    fc.append(send(fpx.at[pl.ds(5, 2), :, pl.ds(128, 128)], fpx.at[pl.ds(7, 2), :, pl.ds(128, 128)], slab_at(-1)))
    fc.append(send(fpx.at[pl.ds(6, 1), :, pl.ds(128, 128)], fpx.at[pl.ds(0, 1), :, pl.ds(128, 128)], slab_at(3)))
    fc.append(send(fpx.at[pl.ds(5, 1), :, pl.ds(128, 128)], fpx.at[pl.ds(11, 1), :, pl.ds(128, 128)], slab_at(-3)))
    fc.append(send(fpx.at[pl.ds(5, 2), :, pl.ds(128, 128)], fpx.at[pl.ds(1, 2), :, pl.ds(128, 128)], slab_at(2)))
    fc.append(send(fpx.at[pl.ds(5, 2), :, pl.ds(128, 128)], fpx.at[pl.ds(9, 2), :, pl.ds(128, 128)], slab_at(-2)))

    banded(w_in, w_a, w_b, w_out, spread[...], wt, w1, w4, wf, tiles, flat, turned)
    for zb in range(NB):
        mask[zb * RY : zb * RY + 72] = jnp.ones((72, 128), F32)
        mask[zb * RY + 72 : zb * RY + RY] = jnp.zeros((8, 128), F32)
    held[3].wait()
    for X in range(2):
        fine, means = parts[X]
        targets = []
        for i, j in stress_pairs:
            t = mean([fine[i][n] * fine[j][n] for n in range(4)]) - means[i] * means[j]
            targets.append(jnp.concatenate([t, blank], axis=0).astype(BF))
        t = mm(jnp.concatenate(targets, axis=1), texp[...])
        for zb in range(8):
            tx[X, zb * RY : zb * RY + RY] = t[:, zb * 128 : zb * 128 + 128]
    pads = jnp.zeros((8, 128), F32)
    for c in range(3):

        @pl.loop(0, 12)
        def _(p, c=c):
            for t in range(2):
                vext[c, p, t, 0:8] = pads
                vext[c, p, t, 152:160] = pads

        @pl.loop(0, 8)
        def _(p, c=c):
            for t in range(2):
                fs[c, p, t, 0:8] = pads
                fs[c, p, t, 152:160] = pads

        for x in range(4):
            vext[c, 4 + x, 0, 8:152] = v[c, x]

    for copy in uc:
        copy.wait_recv()
    vzf[1] = vzr[0] + vzr[1]
    for copy in fc:
        copy.wait_recv()
    odd = lax.rem(s, 2)
    pair = {"slab": s + 1 - 2 * odd}
    beyond = {"slab": lax.rem(s + 2 - 4 * odd + SLAB, SLAB)}
    half = [send(vb, vbx.at[odd], pair), send(vzf.at[1], vzf.at[2 * odd], pair)]

    def expand(src, table, dst, count, shifts, start):
        width = src.shape[2]

        @pl.loop(0, count // 4)
        def _(q):
            r = mm(src[pl.ds(q * 4, 4)].reshape(4 * RY, width), table[...])
            for n in range(4):
                for zb in range(NB):
                    block = r[n * RY : n * RY + RY, zb * 128 : zb * 128 + 128]
                    for m, shift in enumerate(shifts):
                        moved = pltpu.roll(block, shift, 1) if shift else block
                        dst[lax.rem(q * 4 + start, 12) + n, zb * RY : zb * RY + RY, m * 128 : m * 128 + 128] = moved.astype(BF)

    held[2].wait()
    expand(fpx, fexp, xe0, 12, (0, 40, 80), 0)

    @pl.loop(0, 10)
    def _(p):
        write_plane(xe1, p, jnp.tanh(conv_plane(window_fields(xe0, p, ALL), w1[...])) * mask[...])

    for k, (src, dst, count) in enumerate(((xe1, xe2, 8), (xe2, xe3, 6))):

        @pl.loop(0, count)
        def _(p, src=src, dst=dst, k=k):
            write_plane(dst, p, jnp.tanh(conv_plane(window(src, p, ALL), wt[k])) * mask[...])

        if k == 0:
            for copy in half:
                copy.wait_recv()
            vc = [
                send(vbx.at[1 - odd], vbx.at[odd], beyond),
                send(vzf.at[2 - 2 * odd], vzf.at[2 * odd], beyond),
            ]

    held[4].wait()
    held[5].wait()
    for X in range(2):
        pred = conv_plane(window(xe3, X + 1, MID), wt[2]) * mask[MID]
        stress = pred.astype(BF)
        cot = (2.0 / SIZE * (pred - tx[X])).astype(BF)
        c4[X] = cot.astype(F32)
        for value, pack, edges, at in ((cot, cpx, ce, 3), (stress, spx, se, 2)):
            joined = jnp.concatenate([value[zb * RY : zb * RY + RY] for zb in range(8)], axis=1)
            pack[at + X, :, 0:384] = mm(joined, comp[...]).astype(BF)
            edges[0, X] = mm(value[7 * RY : 8 * RY], cedge[0]).astype(BF)
            edges[1, X] = mm(value[0:RY], cedge[1]).astype(BF)

    zc = []
    for side, k in ((0, 1), (1, -1)):
        zc.append(send(ce.at[side], cer.at[side], grp_at(k)))
        zc.append(send(se.at[side], ser.at[side], grp_at(k)))
    cc = []
    cc.append(send(cpx.at[pl.ds(3, 2), :, pl.ds(0, 384)], cpx.at[pl.ds(1, 2), :, pl.ds(0, 384)], slab_at(1)))
    cc.append(send(cpx.at[pl.ds(3, 2), :, pl.ds(0, 384)], cpx.at[pl.ds(5, 2), :, pl.ds(0, 384)], slab_at(-1)))
    cc.append(send(cpx.at[pl.ds(4, 1), :, pl.ds(0, 384)], cpx.at[pl.ds(0, 1), :, pl.ds(0, 384)], slab_at(2)))
    cc.append(send(cpx.at[pl.ds(3, 1), :, pl.ds(0, 384)], cpx.at[pl.ds(7, 1), :, pl.ds(0, 384)], slab_at(-2)))
    weight_gradient(xe3, 1, [c4[0], c4[1]], gsrc, 3, gtmp)

    for copy in zc:
        copy.wait_recv()
    for X in range(2):
        cpx[3 + X, :, 384:512] = cer[0, X] + cer[1, X]
        spx[2 + X, :, 384:512] = ser[0, X] + ser[1, X]
    cc.append(send(cpx.at[pl.ds(3, 2), :, pl.ds(384, 128)], cpx.at[pl.ds(1, 2), :, pl.ds(384, 128)], slab_at(1)))
    cc.append(send(cpx.at[pl.ds(3, 2), :, pl.ds(384, 128)], cpx.at[pl.ds(5, 2), :, pl.ds(384, 128)], slab_at(-1)))
    cc.append(send(cpx.at[pl.ds(4, 1), :, pl.ds(384, 128)], cpx.at[pl.ds(0, 1), :, pl.ds(384, 128)], slab_at(2)))
    cc.append(send(cpx.at[pl.ds(3, 1), :, pl.ds(384, 128)], cpx.at[pl.ds(7, 1), :, pl.ds(384, 128)], slab_at(-2)))

    for copy in vc:
        copy.wait_recv()
    for c in range(3):
        for x in range(4):
            vext[c, x, 0, 8:152] = vbx[0, c, x].astype(F32)
            vext[c, 8 + x, 0, 8:152] = vbx[1, c, x].astype(F32)
    held[8].wait()
    for n in range(3):
        r = mm(vzf[n], vze[...])
        for c in range(3):
            for x in range(4):
                p = c * 4 + x
                vext[c, 4 * n + x, 1, 8:152] = r[:, p * 128 : p * 128 + 128]

    count = 48
    lane = lanes((count, 128))
    low = (lane < 1, lane < 2, lane >= 127, lane >= 126)

    def first_step(start, stop):
        @pl.loop(start, stop)
        def _(p):
            for t in range(2):
                for r in range(0, 144, count):
                    vel, outs = stencil(vext, p + 2, t, r, count, low)
                    for i in range(3):
                        fs[i, p, t, 8 + r : 8 + r + count] = vel[i] + outs[i]

    first_step(0, 3)
    for copy in cc:
        copy.wait_recv()
    sc = []
    sc.append(send(spx.at[pl.ds(2, 2)], spx.at[pl.ds(0, 2)], slab_at(1)))
    sc.append(send(spx.at[pl.ds(2, 2)], spx.at[pl.ds(4, 2)], slab_at(-1)))
    wc = []
    for k in range(1, GRP):
        other = lax.rem(g + k, GRP)
        rows = pl.ds(pl.multiple_of(other * 16, 16), 32)
        wc.append(send(spx.at[pl.ds(2, 2), rows, pl.ds(0, 384)], sw.at[g], grp_at(k)))
    rows = pl.ds(pl.multiple_of(g * 16, 16), 32)
    sw[g] = spx[2:4, rows, 0:384]

    held[6].wait()
    expand(cpx, cexp, xe0, 8, (0, 60), 8)

    def damp(act, p, rows=ALL):
        below = act[p, rows, 0:128].astype(F32)
        return (1.0 - below * below) * mask[rows]

    @pl.loop(0, 6)
    def _(p):
        write_plane(xe3, p, conv_plane(window_cot(xe0, p, ALL), w4[...]) * damp(xe3, p))

    def own(ref, at):
        return [ref[at + X, MID, 0:128].astype(F32) for X in range(2)]

    weight_gradient(xe2, 2, own(xe3, 2), gsrc, 2, gtmp)

    @pl.loop(0, 4)
    def _(p):
        write_plane(xe2, p + 2, conv_plane(window(xe3, p, ALL), wt[3]) * damp(xe2, p + 2))

    weight_gradient(xe1, 3, own(xe2, 3), gsrc, 1, gtmp)
    for X in range(2):
        c1[X] = (conv_plane(window(xe2, X + 2, MID), wt[4]) * damp(xe1, X + 4, MID)).astype(BF).astype(F32)
    first_gradient(xe0, 4, [c1[0], c1[1]], gsrc, gtmp)

    first = [send(gsrc.at[peer_a(k)[0]], r1.at[k - 1], peer_a(k)[1]) for k in range(1, 16)]

    first_step(3, 8)
    for copy in first:
        copy.wait_recv()
    total = gsrc[a]
    for k in range(15):
        total = total + r1[k]
    r2g[b] = total
    second = [send(r2g.at[b], r2g.at[b], peer_b(k)) for k in range(1, 8)]

    for copy in sc:
        copy.wait_recv()
    for n in (9, 10, 11):
        held[n].wait()
    for n in range(8):
        at = 1 + n // 2
        lower, mid, upper = (spx[at + d].astype(F32) for d in (-1, 0, 1))
        if n % 2 == 0:
            slope = 8.0 * mid - upper - 7.0 * lower
        else:
            slope = 7.0 * upper - 8.0 * mid + lower
        gxt[n * RY : n * RY + RY, 0:512] = slope.astype(BF)
        gxt[n * RY : n * RY + RY, 512:1024] = spx[at]
        if n % 2 == 0:
            r2s[n // 2] = mm(spx[at], q2[...]).astype(BF)
    r = mm(gxt[...], q1[...]).astype(BF)
    for n in range(8):
        both = jnp.concatenate([r[n * RY : n * RY + RY], r2s[n // 2]], axis=0)
        force[n] = mm(pb[...], both) * (-4.0 / 12.0)

    for copy in second:
        copy.wait_recv()
    total = r2g[0]
    for k in range(1, 8):
        total = total + r2g[k]
    gout[a] = total
    third = [send(gout.at[a], gout.at[a], peer_a(k)[1]) for k in range(1, 16)]

    @pl.loop(0, 8)
    def _(p):
        for t in range(2):
            for i in range(3):
                at = i * 256 + t * 128
                fs[i, p, t, 8:152] = fs[i, p, t, 8:152] + 0.1 * force[p, :, at : at + 128]

    @pl.loop(0, 4)
    def _(x):
        for r in range(0, 144, count):
            vel, outs = stencil(fs, x + 2, 0, r, count, low)
            for i in range(3):
                again = outs[i] + 0.1 * force[x + 2, r : r + count, i * 256 : i * 256 + 128]
                vnext[i, x, r : r + count] = 0.5 * (v[i, x, r : r + count] + vel[i] + again)

    for copy in third:
        copy.wait_recv()
    for copy in wc:
        copy.wait_recv()
    for copy in sent:
        copy.wait_send()


def finish(vnext, sw, gout, vout, stress, g0, g1, g2, g3, rows, taps):
    vout[...] = vnext[...]
    start = 2 * lax.axis_index("grp")
    low = lanes((18, 128)) < 64
    for tile in range(3):
        rows[tile] = sw[:, :, :, tile * 128 : tile * 128 + 128].astype(F32)
    for c in range(6):
        for half in range(2):
            planes = []
            for x in range(2):
                left = rows[c // 2, 2 * half, x, pl.ds(start, 18), :]
                right = rows[c // 2, 2 * half + 1, x, pl.ds(start, 18), :]
                if c % 2:
                    left = pltpu.roll(left, 64, 1)
                else:
                    right = pltpu.roll(right, 64, 1)
                planes.append(jnp.where(low, left, right))
            stress[c, :, :, half * 128 : half * 128 + 128] = jnp.stack(planes, axis=1).astype(BF)
    for layer, out in enumerate((g0, g1, g2, g3)):
        for tap in range(27):
            tile = gout[layer * 4 + tap // 8]
            shift = (128 - tap % 8 * 16) % 128
            taps[tap * 16 : tap * 16 + 16] = pltpu.roll(tile, shift, 1) if shift else tile
        for n in range(16 if layer == 0 else out.shape[0]):
            turned = jnp.transpose(taps[pl.ds(n, 32, stride=16), :])
            if layer == 0:
                for q in range(3):
                    out[q, n : n + 1] = turned[q : q + 1, 0:27]
            else:
                out[n] = turned[0:16, 0:27]


def local(velocity, w_in, w_mid_a, w_mid_b, w_out):
    vm = pltpu.VMEM
    scratch = [
        vm((12, RY, 256), BF), vm((2, 2, RY, 128), BF), vm((2, 2, RY, 128), BF),
        vm((3, 4, 144, 128), BF), vm((2, 3, 4, 144, 128), BF),
        vm((2, 144, 128), BF), vm((2, 144, 128), BF), vm((3, 144, 128), BF),
        vm((2, OWN, 128), F32), vm((5, 512, 384), BF),
        vm((128, 384), BF), vm((256, 384), BF), vm((256, 384), F32), vm((27, 16, 128), F32),
        vm((256, 128), F32), vm((512, 128), F32),
        vm((12, ROWS, 384), BF), vm((10, ROWS, 512), BF), vm((8, ROWS, 512), BF), vm((6, ROWS, 512), BF),
        vm((2, OWN, 128), F32),
        vm((2, OWN, 128), F32),
        vm((ROWS, 128), F32),
        vm((8, RY, 512), BF), vm((6, RY, 512), BF),
        vm((2, 2, RY, 128), BF), vm((2, 2, RY, 128), BF), vm((2, 2, RY, 128), BF), vm((2, 2, RY, 128), BF),
        vm((8 * RY, 1024), BF), vm((4, RY, 768), BF), vm((8, 144, 768), F32),
        vm((3, 12, 2, 160, 128), F32), vm((3, 8, 2, 160, 128), F32),
        vm((384, 512), F32), vm((16, 16, 128), F32), vm((15, 16, 128), F32), vm((8, 16, 128), F32),
        pltpu.SemaphoreType.DMA((12,)), pltpu.SemaphoreType.DMA((80,)), pltpu.SemaphoreType.DMA((80,)),
    ]
    *consts, spread = tables()
    scratch = [vm(t.shape, BF) for t in consts] + scratch
    inside = pl.BlockSpec(memory_space=pltpu.VMEM)
    vnext, sw, gout = pl.pallas_call(
        body,
        out_shape=[
            jax.ShapeDtypeStruct((3, 4, 144, 128), F32),
            jax.ShapeDtypeStruct((4, 2, 32, 384), BF),
            jax.ShapeDtypeStruct((16, 16, 128), F32),
        ],
        in_specs=[inside] * 6 + [pl.BlockSpec(memory_space=pl.ANY)] * len(consts),
        out_specs=[inside] * 3,
        scratch_shapes=scratch,
        compiler_params=pltpu.CompilerParams(
            collective_id=0, has_side_effects=True, vmem_limit_bytes=62 * 1024 * 1024
        ),
    )(
        velocity,
        jnp.transpose(w_in, (2, 1, 0)),
        *(jnp.transpose(w, (1, 2, 0)) for w in (w_mid_a, w_mid_b, w_out)),
        spread,
        *consts,
    )
    shapes = [((3, 4, 144, 128), F32), ((6, 18, 2, 256), BF)]
    shapes += [((3, 16, 27), F32), ((16, 16, 27), F32), ((16, 16, 27), F32), ((6, 16, 27), F32)]
    vnext, stress, g0, *rest = pl.pallas_call(
        finish,
        out_shape=[jax.ShapeDtypeStruct(*shape) for shape in shapes],
        in_specs=[inside] * 3,
        out_specs=[inside] * 6,
        scratch_shapes=[vm((3, 4, 2, 32, 128), F32), vm((512, 128), F32)],
        compiler_params=pltpu.CompilerParams(vmem_limit_bytes=60 * 1024 * 1024),
    )(vnext, sw, gout)
    stress = jnp.transpose(stress, (0, 2, 1, 3))
    return (vnext, stress, jnp.transpose(g0, (2, 1, 0)), *(jnp.transpose(g, (2, 0, 1)) for g in rest))


def solution(mesh):
    in_specs = (P(None, "slab", None, "grp"), P(), P(), P(), P())
    out_specs = (P(None, "slab", None, "grp"), P(None, "slab", "grp", None), P(), P(), P(), P())
    return jax.shard_map(local, mesh=mesh, in_specs=in_specs, out_specs=out_specs, check_vma=False)
```
